256 devices in a mesh: leaf: 64 (over y, z, core), tensor: 4 (over x).
Axes of the slice: x: 4, y: 4, z: 8, core: 2. Of those that a mesh axis runs over, the one named last changes fastest.
Arguments:
- queries: bfloat16 [2048, 32, 2048], P('leaf', None, 'tensor'), may hold values from -6 to 6
- keys: bfloat16 [2048, 32, 512], P('leaf', None, 'tensor'), may hold values from -6 to 6
- values: bfloat16 [2048, 32, 512], P('leaf', None, 'tensor'), may hold values from -6 to 6
- resid: bfloat16 [2048, 32, 4096], P('leaf', None, 'tensor'), may hold values from -6 to 6
- out_weight: bfloat16 [2048, 4096], P('tensor'), may hold values from -0.125 to 0.125
- norm_gain: bfloat16 [4096], P('tensor'), may hold values from 0.5 to 1.5
- value_weight: bfloat16 [4096], P('tensor'), may hold values from -0.09375 to 0.09375
- parent: int32 [2048], P('leaf'), may hold values from -1 to 2047, as said below
- counts: int32 [64], P('leaf'), may hold values from 25 to 32, as said below
Outputs:
- layer_out: bfloat16 [2048, 32, 4096], P('leaf', None, 'tensor')
- backed: float32 [2048], P('leaf')
The draws below stay inside these ranges and needn't reach their ends.
Inputs may be any that keep to these rules, and one draw needn't show every extreme that they name: parent[n] is -1 for nodes of level 0 and for nodes that are not live; otherwise it is a live node of level one less. The parents of one device's nodes that lie on other devices lie on distinct devices. `counts`: every device holds at least 3 full levels.
All inputs are finite; a program needn't handle non-finite values.
Results may differ from the reference program's by a relative error of at most 0.008.
Values may be sent and summed in bfloat16 or wider, within the bound.
A program may use at most 128 MiB of HBM per device.

```python
import math
import jax
import jax.numpy as jnp
from jax import lax

D = 4096
HEADS = 16
KV_HEADS = 4
DH = 128
BLK = 32
LEVELS = 4
W = 8
NB_DEV = 32
NODES = 2048
N_LEAF = 64


def tree_counts(key):
    key = jax.random.fold_in(key, 101)
    counts_low = jax.random.randint(key, (N_LEAF,), (LEVELS - 1) * W + 1, LEVELS * W + 1)
    full_device = jax.random.randint(jax.random.fold_in(key, 1), (), 0, N_LEAF)
    return jnp.where(jnp.arange(N_LEAF) == full_device, LEVELS * W, counts_low).astype(jnp.int32)


def draw_counts(key, part):
    return tree_counts(key)


def draw_parent(key, part):
    counts_all = tree_counts(key)
    key = jax.random.fold_in(key, 7)
    slot_count = LEVELS * W
    device_keys = jax.random.split(jax.random.fold_in(key, 1), N_LEAF)
    peer_orders = jax.vmap(lambda subkey: jax.random.permutation(subkey, N_LEAF - 1))(device_keys)
    device = jnp.arange(N_LEAF)[:, None]
    slot_ids = jnp.arange(slot_count)[None, :]
    node_level = slot_ids // W
    within = slot_ids % W
    position = jnp.clip((node_level - 1) * W + within, 0, N_LEAF - 2)
    position = jnp.broadcast_to(position, (N_LEAF, slot_count))
    peer_dev = (device + 1 + jnp.take_along_axis(peer_orders, position, axis=1)) % N_LEAF
    remote = jax.random.randint(jax.random.fold_in(key, 2), (N_LEAF, slot_count), 0, 8) > 0
    remote = remote | (slot_ids == W)
    pick_slot = jax.random.randint(jax.random.fold_in(key, 3), (N_LEAF, slot_count), 0, W)
    owner_dev = jnp.where(remote, peer_dev, device)
    target = owner_dev * slot_count + (node_level - 1) * W + pick_slot
    alive_slot = slot_ids < counts_all[:, None]
    result = jnp.where((node_level >= 1) & alive_slot, target, -1)
    return result.reshape(-1).astype(jnp.int32)


def draw_queries(key, part):
    key = jax.random.fold_in(key, 11)
    array_shape = (NODES, BLK, HEADS * DH)
    entries = jnp.clip(jax.random.normal(key, array_shape, jnp.float32), -6.0, 6.0)
    return entries.astype(jnp.bfloat16)


def draw_keys(key, part):
    key = jax.random.fold_in(key, 13)
    array_shape = (NODES, BLK, KV_HEADS * DH)
    entries = jnp.clip(jax.random.normal(key, array_shape, jnp.float32), -6.0, 6.0)
    return entries.astype(jnp.bfloat16)


def block_scale(rng, extent, cuts, smallest, high):
    factor_of = 1.0
    for dim, shards_of in cuts:
        draws = jax.random.uniform(jax.random.fold_in(jax.random.fold_in(rng, 6), dim), (shards_of,), jnp.float32, smallest / len(cuts), high / len(cuts))
        factor_of = factor_of * jnp.repeat(jnp.exp(draws), extent[dim] // shards_of).reshape((-1,) + (1,) * (len(extent) - 1 - dim))
    return factor_of


def centred(key, dims, spread, limit, cuts=(), kind=jnp.bfloat16):
    factor_of = block_scale(key, dims, cuts, -0.22, 0.18) if cuts else 1.0
    array = jax.random.normal(key, dims, jnp.float32) * spread * factor_of
    return jnp.minimum(jnp.maximum(array, -limit), limit).astype(kind)


def setup_inputs(seed: int = 0) -> dict:
    key_of = jax.random.split(jax.random.key(seed), 10)
    return {
        "queries": draw_queries(jax.random.fold_in(key_of[9], 71), 0),
        "keys": draw_keys(jax.random.fold_in(key_of[9], 71), 0),
        "values": centred(key_of[2], (NODES, BLK, KV_HEADS * DH), 1.0, 6.0, ((0, 64), (2, 4))),
        "resid": centred(key_of[3], (NODES, BLK, D), 1.0, 6.0, ((0, 64), (2, 4))),
        "out_weight": centred(key_of[4], (HEADS * DH, D), (HEADS * DH) ** -0.5, 0.125, ((0, 4),)),
        "norm_gain": jnp.clip(1.0 + 0.1 * jax.random.normal(key_of[5], (D,), jnp.float32), 0.5, 1.5).astype(jnp.bfloat16),
        "value_weight": centred(key_of[6], (D,), D ** -0.5, 0.09375, ((0, 4),)),
        "parent": draw_parent(jax.random.fold_in(key_of[9], 71), 0),
        "counts": draw_counts(jax.random.fold_in(key_of[9], 71), 0),
    }


norm_eps = 1e-05
masked_score = -1e+30

def climb(parent, node_ids):
    clipped = jnp.clip(node_ids, 0, parent.shape[0] - 1)
    return jnp.where(node_ids >= 0, parent[clipped], -1).astype(jnp.int32)

def fetch_rows(source_rows, node_ids):
    clipped = jnp.clip(node_ids, 0, source_rows.shape[0] - 1)
    taken = source_rows[clipped]
    return jnp.where((node_ids >= 0)[:, None, None], taken, jnp.zeros_like(taken))

def reference(queries, keys, values, resid, out_weight, norm_gain, value_weight, parent, counts):
    node_total = parent.shape[0]
    all_ids = jnp.arange(node_total, dtype=jnp.int32)
    slot_ids = all_ids % NB_DEV
    node_level = slot_ids // W
    alive_node = slot_ids < counts[all_ids // NB_DEV]
    kv_rows = jnp.concatenate((keys, values), axis=2)
    head_cols = HEADS * DH
    kv_cols = KV_HEADS * DH
    group = HEADS // KV_HEADS
    key_slot = jnp.arange(LEVELS * BLK, dtype=jnp.int32)
    distance = LEVELS - 1 - key_slot // BLK
    query_slot = jnp.arange(BLK, dtype=jnp.int32)
    causal = (distance[None, :] == 0) & (key_slot[None, :] % BLK <= query_slot[:, None])
    mixer = norm_gain.astype(jnp.float32) * value_weight.astype(jnp.float32)

    def node_group(start):
        group_ids = start + jnp.arange(NB_DEV, dtype=jnp.int32)
        current = group_ids
        fetched = []
        for hop in range(LEVELS - 1):
            current = climb(parent, current)
            fetched.append(fetch_rows(kv_rows, current))
        own_rows = lax.dynamic_slice_in_dim(kv_rows, start, NB_DEV, 0)
        context = jnp.concatenate(fetched[::-1] + [own_rows], axis=1)
        level_group = lax.dynamic_slice_in_dim(node_level, start, NB_DEV, 0)
        alive_group = lax.dynamic_slice_in_dim(alive_node, start, NB_DEV, 0)
        ancestor_ok = (distance[None, :] >= 1) & (distance[None, :] <= level_group[:, None])
        allowed = ancestor_ok[:, None, None, None, :] | causal[None, None, None, :, :]
        query_heads = lax.dynamic_slice_in_dim(queries, start, NB_DEV, 0).astype(jnp.float32)
        query_heads = query_heads.reshape(NB_DEV, BLK, KV_HEADS, group, DH)
        key_heads = context[:, :, :kv_cols].astype(jnp.float32).reshape(NB_DEV, LEVELS * BLK, KV_HEADS, DH)
        value_heads = context[:, :, kv_cols:].astype(jnp.float32).reshape(NB_DEV, LEVELS * BLK, KV_HEADS, DH)
        scores = jnp.einsum('nqgrd,nkgd->ngrqk', query_heads, key_heads) * DH ** (-0.5)
        scores = jnp.where(allowed, scores, masked_score)
        highest = lax.optimization_barrier(jnp.max(scores, axis=-1, keepdims=True))
        expo = jnp.exp(scores - highest)
        weights = (expo / lax.optimization_barrier(jnp.sum(expo, axis=-1, keepdims=True))).astype(jnp.bfloat16)
        attended = jnp.einsum('ngrqk,nkgd->nqgrd', weights.astype(jnp.float32), value_heads)
        attended = attended.astype(jnp.bfloat16).reshape(NB_DEV * BLK, head_cols)
        projected = jnp.dot(attended, out_weight, preferred_element_type=jnp.float32)
        resid_rows = lax.dynamic_slice_in_dim(resid, start, NB_DEV, 0).reshape(NB_DEV * BLK, D)
        hidden = (resid_rows.astype(jnp.float32) + projected).astype(jnp.bfloat16)
        hidden_f = hidden.astype(jnp.float32)
        squares = lax.optimization_barrier(jnp.sum(hidden_f * hidden_f, axis=-1))
        mixed = lax.optimization_barrier(jnp.sum(hidden_f * mixer, axis=-1))
        token_score = mixed / jnp.sqrt(squares / D + norm_eps)
        reward = jnp.tanh(lax.optimization_barrier(jnp.sum(token_score.reshape(NB_DEV, BLK), axis=1)) / math.sqrt(BLK))
        reward = jnp.where(alive_group, reward, 0.0)
        hidden_out = jnp.where(alive_group[:, None, None], hidden.reshape(NB_DEV, BLK, D), jnp.zeros((NB_DEV, BLK, D), jnp.bfloat16))
        return (hidden_out, reward)
    starts = jnp.arange(node_total // NB_DEV, dtype=jnp.int32) * NB_DEV
    layer_out, rewards = lax.map(node_group, starts)
    layer_out = layer_out.reshape(node_total, BLK, D)
    rewards = rewards.reshape(node_total)
    has_parent = parent >= 0
    clipped = jnp.clip(parent, 0, node_total - 1)
    child_count = jax.ops.segment_sum(has_parent.astype(jnp.int32), clipped, num_segments=node_total)
    backed = rewards
    for hop in range(LEVELS - 1):
        target_level = LEVELS - 2 - hop
        child_sum = jax.ops.segment_sum(jnp.where(has_parent, backed, 0.0), clipped, num_segments=node_total)
        divisor = jnp.maximum(child_count, 1).astype(rewards.dtype)
        updated = jnp.where(child_count > 0, 0.5 * rewards + 0.5 * child_sum / divisor, rewards)
        backed = jnp.where(node_level == target_level, updated, backed)
    return (layer_out, backed)
```

```python
import math

import jax
import jax.numpy as jnp
from jax import lax
from jax.experimental import pallas as pl
from jax.experimental.pallas import tpu as pltpu
from jax.sharding import PartitionSpec as P

D = 4096
DH = 128
BLK = 32
LEVELS = 4
W = 8
NX, NY, NZ, NC = 4, 4, 8, 2
ZC = NZ * NC
SLOTS = LEVELS * W
HEADS_HERE = 4
ROWS = W * BLK
COLS = HEADS_HERE * DH
WIDTH = D // NX
WROWS = COLS // (NY * NC)
TILE = 256
HALF = W // 2
BATCHES = ((0, 1), (0, 2), (1, 2), (0, 3), (1, 3), (2, 3))

norm_eps = 1e-05
masked_score = -1e30
BF16 = jnp.bfloat16
F32 = jnp.float32
MESH = pl.DeviceIdType.MESH


def kernel(
    q_hbm, k_hbm, v_hbm, r_hbm, w_hbm, gain_ref, vw_ref, ptile_ref, counts_ref,
    hid_hbm, bk_ref,
    q_v, k_v, v_v, r_v, wf, kvg0, kvg1, kvg2, ag, ysa, ysp, ysm, yh, yr, hid_v,
    gp, ap, gr, ar, psm, pvm, amat, bmat, invm, keepm, stats, srecv, rtile, sqacc, mxacc,
    lsem, zs, zr, sbs, sbr, yas, yar, yfs, yfr, xs, xr, wxs, wxr, wys, wyr, wbs, wbr,
    g1s, g1r, g2s, g2r, sts, strv,
):
    kvg = (kvg0, kvg1, kvg2)
    leaf = lax.axis_index("leaf")
    x = lax.axis_index("tensor")
    c = lax.rem(leaf, NC)
    z = lax.rem(leaf // NC, NZ)
    y = leaf // ZC
    zc = lax.rem(leaf, ZC)

    def leaf_of(yy, zz, cc):
        return (yy * NZ + zz) * NC + cc

    def shift(v, d, n):
        return lax.rem(v + d + n, n)

    yp, ym, ya2 = shift(y, 1, NY), shift(y, -1, NY), shift(y, 2, NY)
    xp, xm, xa = shift(x, 1, NX), shift(x, -1, NX), shift(x, 2, NX)
    zp, zm = shift(z, 1, NZ), shift(z, -1, NZ)
    at_zp, at_zm = (leaf_of(y, zp, c), x), (leaf_of(y, zm, c), x)
    at_sib = (leaf_of(y, z, 1 - c), x)
    at_yp, at_ym, at_ya = (leaf_of(yp, z, c), x), (leaf_of(ym, z, c), x), (leaf_of(ya2, z, c), x)
    at_xp, at_xm, at_xa = (leaf, xp), (leaf, xm), (leaf, xa)

    def plane_peer(i):
        return (y * ZC + lax.rem(zc + i, ZC), x)

    started = []

    def remote(src, dst, ssem, rsem, dev):
        copy = pltpu.make_async_remote_copy(
            src_ref=src, dst_ref=dst, send_sem=ssem, recv_sem=rsem, device_id=dev, device_id_type=MESH
        )
        return copy

    def send(src, dst, ssem, rsem, dev):
        copy = remote(src, dst, ssem, rsem, dev)
        copy.start()
        started.append(copy)

    def arrived(ref, ssem, rsem):
        remote(ref, ref, ssem, rsem, at_sib).wait_recv()

    barrier = pltpu.get_barrier_semaphore()
    partners = [plane_peer(i) for i in range(1, ZC)] + [at_yp, at_ym, at_ya, at_xp, at_xm, at_xa]
    for dev in partners:
        pl.semaphore_signal(barrier, inc=1, device_id=dev, device_id_type=MESH)

    locals_ = []

    def local(src, dst):
        copy = pltpu.make_async_copy(src, dst, lsem.at[len(locals_)])
        copy.start()
        locals_.append(copy)
        return copy

    own_kv = []
    for l in range(3):
        own_kv.append(
            (
                local(k_hbm.at[pl.ds(W * l, W)], kvg[l].at[zc, 0]),
                local(v_hbm.at[pl.ds(W * l, W)], kvg[l].at[zc, 1]),
            )
        )
    in_q = local(q_hbm, q_v)
    in_k = local(k_hbm, k_v)
    in_v = local(v_hbm, v_v)
    in_w = local(w_hbm.at[:, pl.ds(pl.multiple_of(x * WIDTH, WIDTH), WIDTH)], wf.at[3])
    in_r = local(r_hbm, r_v)
    pl.semaphore_wait(barrier, len(partners))

    def gather_send(tile, buf, which):
        for i in range(1, ZC):
            send(tile, buf.at[zc], g1s.at[which, i], g1r.at[which, i], plane_peer(i))

    def gather_pass(tile, buf, whole, which):
        buf[zc] = tile[...]
        for i in range(1, ZC):
            arrived(buf.at[lax.rem(zc + ZC - i, ZC)], g1s.at[which, i], g1r.at[which, i])
        for half in range(2):
            total = buf[8 * half]
            for i in range(1, 8):
                total = total + buf[8 * half + i]
            whole[y, half] = total
        send(whole.at[y], whole.at[y], g2s.at[which, 0], g2r.at[which, 0], at_yp)
        send(whole.at[y], whole.at[y], g2s.at[which, 1], g2r.at[which, 1], at_ym)
        send(whole.at[y], whole.at[y], g2s.at[which, 2], g2r.at[which, 2], at_ya)

    def gather_end(whole, which):
        arrived(whole.at[ym], g2s.at[which, 0], g2r.at[which, 0])
        arrived(whole.at[yp], g2s.at[which, 1], g2r.at[which, 1])
        arrived(whole.at[ya2], g2s.at[which, 2], g2r.at[which, 2])

    def zidx(d, cc):
        return shift(z, d, NZ) * NC + cc

    def z_start(l):
        for copy in own_kv[l]:
            copy.wait()
        own = kvg[l].at[zc]
        send(own, own, zs.at[l, 0, 0], zr.at[l, 0, 0], at_zp)
        send(own, own, zs.at[l, 1, 0], zr.at[l, 1, 0], at_zm)
        send(own, own, sbs.at[l, 0], sbr.at[l, 0], at_sib)

    def z_step(l, s):
        for way, d in ((0, -s), (1, s)):
            shard = kvg[l].at[zidx(d, c)]
            part = shard if s < 4 else shard.at[way]
            arrived(part, zs.at[l, way, s - 1], zr.at[l, way, s - 1])
            if s < 4:
                onward = shard if s < 3 else shard.at[way]
                send(onward, onward, zs.at[l, way, s], zr.at[l, way, s], at_zm if way else at_zp)
                send(shard, shard, sbs.at[l, 1 + way * 3 + s - 1], sbr.at[l, 1 + way * 3 + s - 1], at_sib)
        if s == 4:
            shard = kvg[l].at[zidx(4, c)]
            send(shard, shard, sbs.at[l, 7], sbr.at[l, 7], at_sib)

    def z_end(l):
        for j, d in enumerate((0, -1, -2, -3, 1, 2, 3, 4)):
            arrived(kvg[l].at[zidx(d, 1 - c)], sbs.at[l, j], sbr.at[l, j])

    def climb(node, hops):
        for _ in range(hops):
            node = jnp.maximum(psm[lax.shift_right_logical(node, 5), node & 31], 0)
        return node

    def locate(dev, l, n, s):
        node = climb(dev * SLOTS + W * l + n, l - s)
        owner = lax.shift_right_logical(node, 5)
        return lax.shift_right_logical(owner, 4), owner & 15, node & 7

    def y_far(b):
        s, l = BATCHES[b]
        dev = ya2 * ZC + zc

        def pick(n, carry):
            _, src, slot = locate(dev, l, n, s)
            for kv in range(2):
                ysa[b, n, kv] = kvg[s][src, kv, slot]
            return carry

        lax.fori_loop(0, W, pick, 0)
        first, second = ysa.at[b, pl.ds(0, HALF)], ysa.at[b, pl.ds(HALF, HALF)]
        send(first, yh.at[b, 0], yas.at[b, 0], yar.at[b, 0], at_yp)
        send(second, yh.at[b, 1], yas.at[b, 1], yar.at[b, 1], at_ym)

    def y_near(b):
        s, l = BATCHES[b]
        arrived(yh.at[b, 0], yas.at[b, 0], yar.at[b, 0])
        arrived(yh.at[b, 1], yas.at[b, 1], yar.at[b, 1])
        dev_p = yp * ZC + zc
        dev_m = ym * ZC + zc

        def pick(n, carry):
            for half in range(2):
                row = half * HALF + n
                for out, dev, way in ((ysp, dev_p, 0), (ysm, dev_m, 1)):
                    col, src, slot = locate(dev, l, row, s)
                    for kv in range(2):
                        mine = kvg[s][src, kv, slot]
                        if half == way:
                            mine = jnp.where(col == y, mine, yh[b, way, n, kv])
                        out[b, row, kv] = mine
            return carry

        lax.fori_loop(0, HALF, pick, 0)
        send(ysp.at[b], yr.at[b, 0], yfs.at[b, 0], yfr.at[b, 0], at_yp)
        send(ysm.at[b], yr.at[b, 1], yfs.at[b, 1], yfr.at[b, 1], at_ym)

    def y_end(b):
        arrived(yr.at[b, 0], yfs.at[b, 0], yfr.at[b, 0])
        arrived(yr.at[b, 1], yfs.at[b, 1], yfr.at[b, 1])

    row_q = lax.broadcasted_iota(jnp.int32, (HEADS_HERE * BLK, LEVELS * BLK), 0) & (BLK - 1)
    key_j = lax.broadcasted_iota(jnp.int32, (HEADS_HERE * BLK, LEVELS * BLK), 1)

    def attention(l):
        allowed = ((key_j < BLK) & (key_j <= row_q)) | ((key_j >= BLK) & (key_j < BLK * (l + 1)))
        mine_dev = leaf

        def one(n, half):
            node = W * l + n
            q_node = q_v[node]
            q_rows = jnp.concatenate([q_node[:, h * DH : (h + 1) * DH] for h in range(HEADS_HERE)], axis=0)
            parts = [[k_v[node]], [v_v[node]]]
            for k in range(1, l + 1):
                s = l - k
                b = BATCHES.index((s, l))
                col, src, slot = locate(mine_dev, l, n, s)
                here = col == y
                if half == 0:
                    from_p = col == yp
                else:
                    from_p = jnp.logical_not(here | (col == ym))
                for kv in range(2):
                    block = jnp.where(from_p, yr[b, 1, n, kv], yr[b, 0, n, kv])
                    block = jnp.where(here, kvg[s][src, kv, slot], block)
                    parts[kv].append(block)
            for kv in range(2):
                for _ in range(l + 1, LEVELS):
                    parts[kv].append(jnp.zeros((BLK, DH), BF16))
            k_all = jnp.concatenate(parts[0], axis=0)
            v_all = jnp.concatenate(parts[1], axis=0)
            scores = lax.dot_general(
                q_rows, k_all, (((1,), (1,)), ((), ())), preferred_element_type=F32
            ) * DH ** (-0.5)
            scores = jnp.where(allowed, scores, masked_score)
            highest = jnp.max(scores, axis=1, keepdims=True)
            expo = jnp.exp(scores - highest)
            weights = (expo / jnp.sum(expo, axis=1, keepdims=True)).astype(BF16)
            got = jnp.dot(weights, v_all, preferred_element_type=F32).astype(BF16)
            rows = pl.ds(pl.multiple_of(n * BLK, BLK), BLK)
            for h in range(HEADS_HERE):
                ag[3, l, rows, h * DH : (h + 1) * DH] = got[h * BLK : (h + 1) * BLK]

        for half in range(2):

            def pair(i, carry):
                for j in range(2):
                    one(half * HALF + 2 * i + j, half)
                return carry

            lax.fori_loop(0, HALF // 2, pair, 0)
        own = ag.at[3, l]
        send(own, ag.at[0, l], xs.at[l, 0], xr.at[l, 0], at_xp)
        send(own, ag.at[1, l], xs.at[l, 1], xr.at[l, 1], at_xm)

    def x_pass(l):
        top, low = pl.ds(0, ROWS // 2), pl.ds(ROWS // 2, ROWS // 2)
        arrived(ag.at[0, l], xs.at[l, 0], xr.at[l, 0])
        send(ag.at[0, l, top], ag.at[2, l, top], xs.at[l, 2], xr.at[l, 2], at_xp)
        arrived(ag.at[1, l], xs.at[l, 1], xr.at[l, 1])
        send(ag.at[1, l, low], ag.at[2, l, low], xs.at[l, 3], xr.at[l, 3], at_xm)

    def x_end(l):
        arrived(ag.at[2, l, pl.ds(0, ROWS // 2)], xs.at[l, 2], xr.at[l, 2])
        arrived(ag.at[2, l, pl.ds(ROWS // 2, ROWS // 2)], xs.at[l, 3], xr.at[l, 3])

    def w_rows(yy, cc):
        return pl.ds(pl.multiple_of((yy * NC + cc) * WROWS, WROWS), WROWS)

    def w_start():
        rows = w_rows(y, c)
        for slot, to, dev in ((0, xp, at_xp), (1, xm, at_xm), (2, xa, at_xa)):
            cols = pl.ds(pl.multiple_of(to * WIDTH, WIDTH), WIDTH)
            send(w_hbm.at[rows, cols], wf.at[slot, rows], wxs.at[slot], wxr.at[slot], dev)

    three = pl.ds(0, 3)

    def w_mid():
        rows = w_rows(y, c)
        for slot in range(3):
            arrived(wf.at[slot, rows], wxs.at[slot], wxr.at[slot])
        piece = wf.at[three, rows]
        send(piece, piece, wys.at[0], wyr.at[0], at_yp)
        send(piece, piece, wys.at[1], wyr.at[1], at_ym)
        send(piece, piece, wbs.at[0], wbr.at[0], at_sib)

    def w_halves(yy, cc):
        base = (yy * NC + cc) * WROWS
        return (
            pl.ds(pl.multiple_of(base, WROWS // 2), WROWS // 2),
            pl.ds(pl.multiple_of(base + WROWS // 2, WROWS // 2), WROWS // 2),
        )

    def w_pass():
        for j, (yy, dev) in enumerate(((ym, at_yp), (yp, at_ym))):
            piece = wf.at[three, w_rows(yy, c)]
            arrived(piece, wys.at[j], wyr.at[j])
            onward = wf.at[three, w_halves(yy, c)[j]]
            send(onward, onward, wys.at[2 + j], wyr.at[2 + j], dev)
            send(piece, piece, wbs.at[1 + j], wbr.at[1 + j], at_sib)

    def w_last():
        for j in range(2):
            arrived(wf.at[three, w_halves(ya2, c)[j]], wys.at[2 + j], wyr.at[2 + j])
        piece = wf.at[three, w_rows(ya2, c)]
        send(piece, piece, wbs.at[3], wbr.at[3], at_sib)

    def w_end():
        for j, yy in enumerate((y, ym, yp, ya2)):
            arrived(wf.at[three, w_rows(yy, 1 - c)], wbs.at[j], wbr.at[j])
        in_w.wait()

    out_copies = []

    def project(l):
        sqacc[...] = jnp.zeros_like(sqacc)
        mxacc[...] = jnp.zeros_like(mxacc)

        def tile(j, carry):
            cols = pl.ds(pl.multiple_of(j * TILE, TILE), TILE)
            total = jnp.dot(ag[3, l], wf[3, :, cols], preferred_element_type=F32)
            for slot in range(3):
                total = total + jnp.dot(ag[slot, l], wf[slot, :, cols], preferred_element_type=F32)
            res = r_v[pl.ds(W * l, W), :, cols].reshape(ROWS, TILE)
            hid = (res.astype(F32) + total).astype(BF16)
            hid_v[pl.ds(W * l, W), :, cols] = hid.reshape(W, BLK, TILE)
            hid_f = hid.astype(F32)
            mixer = gain_ref[:, cols].astype(F32) * vw_ref[:, cols].astype(F32)
            square = hid_f * hid_f
            mixed = hid_f * mixer
            sqacc[...] += square[:, :128] + square[:, 128:]
            mxacc[...] += mixed[:, :128] + mixed[:, 128:]
            return carry

        lax.fori_loop(0, WIDTH // TILE, tile, 0)
        copy = local(hid_v.at[pl.ds(W * l, W)], hid_hbm.at[pl.ds(W * l, W)])
        out_copies.append(copy)
        for base, acc in ((0, sqacc), (8, mxacc)):
            for half in range(2):
                turned = acc[half * 128 : (half + 1) * 128].T
                stats[base + 2 * l + half : base + 2 * l + half + 1, :] = jnp.sum(turned, axis=0, keepdims=True)

    def family():
        parents = ap[...].reshape(NY * ZC, 128)
        pvm[0:64] = parents
        pvm[64:128] = jnp.full((64, 128), -1, jnp.int32)
        turned = pvm[...].T
        pd = lax.broadcasted_iota(jnp.int32, (64, 128), 0)
        lane = lax.broadcasted_iota(jnp.int32, (128, 128), 1)
        for l in range(3):
            for j in range(W):
                child = W * (l + 1) + j
                row = lax.shift_right_arithmetic(turned[child : child + 1, :], 5)
                amat[l, :, j * 128 : (j + 1) * 128] = jnp.where(
                    jnp.broadcast_to(row, (64, 128)) == pd, 1.0, 0.0
                ).astype(BF16)
                col = pvm[:, child : child + 1] & 31
                bmat[l, j * 128 : (j + 1) * 128, :] = jnp.where(
                    jnp.broadcast_to(col, (128, 128)) == lane, 1.0, 0.0
                )
            count = jnp.dot(amat[l], bmat[l].astype(BF16), preferred_element_type=F32)
            invm[l] = jnp.where(count > 0, 0.5 / jnp.maximum(count, 1.0), 0.0)
            keepm[l] = jnp.where(count > 0, 0.5, 1.0)

    def tail():
        for i, dev in enumerate((at_xp, at_xm, at_xa)):
            send(stats, srecv.at[i], sts.at[i], strv.at[i], dev)
        for i in range(3):
            arrived(srecv.at[i], sts.at[i], strv.at[i])
        total = (stats[...] + srecv[0]) + (srecv[1] + srecv[2])
        score = total[8:16] / jnp.sqrt(total[0:8] / D + norm_eps)
        jj = lax.broadcasted_iota(jnp.int32, (128, 128), 0)
        nn = lax.broadcasted_iota(jnp.int32, (128, 128), 1)
        group = jnp.where((jj // BLK) == (nn & 3), 1.0, 0.0)
        sums = jnp.dot(score, group, preferred_element_type=F32, precision=lax.Precision.HIGHEST)
        rr = lax.broadcasted_iota(jnp.int32, (8, 128), 0)
        ln = lax.broadcasted_iota(jnp.int32, (8, 128), 1)
        per_node = jnp.sum(jnp.where((ln // 4) == rr, sums, 0.0), axis=0, keepdims=True)
        reward = jnp.tanh(per_node / math.sqrt(BLK))
        wide = jnp.broadcast_to(reward, (8, 128))
        rtile[...] = jnp.where((rr == (zc & 7)) & (ln < counts_ref[0]), wide, 0.0)
        gather_send(rtile, gr, 1)
        gather_pass(rtile, gr, ar, 1)
        gather_end(ar, 1)
        values = ar[...].reshape(NY * ZC, 128)
        for l in (2, 1, 0):
            padded = jnp.concatenate([values, jnp.zeros((64, 128), F32)], axis=0)
            spread = jnp.concatenate(
                [
                    bmat[l, j * 128 : (j + 1) * 128, :]
                    * jnp.broadcast_to(padded[:, W * (l + 1) + j : W * (l + 1) + j + 1], (128, 128))
                    for j in range(W)
                ],
                axis=0,
            )
            high = spread.astype(BF16)
            rest = spread - high.astype(F32)
            mid = rest.astype(BF16)
            low = (rest - mid.astype(F32)).astype(BF16)
            summed = jnp.dot(amat[l], high, preferred_element_type=F32)
            summed = summed + jnp.dot(amat[l], mid, preferred_element_type=F32)
            summed = summed + jnp.dot(amat[l], low, preferred_element_type=F32)
            values = keepm[l] * values + invm[l] * summed
        who = lax.broadcasted_iota(jnp.int32, (64, 128), 0)
        bk_ref[...] = jnp.sum(jnp.where(who == leaf, values, 0.0), axis=0, keepdims=True)

    gather_send(ptile_ref, gp, 0)
    z_start(0)
    w_start()
    z_start(1)
    in_q.wait()
    in_k.wait()
    in_v.wait()
    attention(0)
    z_step(0, 1)
    gather_pass(ptile_ref, gp, ap, 0)
    z_step(1, 1)
    w_mid()
    z_step(0, 2)
    z_start(2)
    z_step(1, 2)
    z_step(0, 3)
    gather_end(ap, 0)
    pvm[0:64] = ap[...].reshape(NY * ZC, 128)
    to_smem = local(pvm.at[pl.ds(0, 64)], psm)
    z_step(1, 3)
    x_pass(0)
    z_step(0, 4)
    z_step(2, 1)
    w_pass()
    to_smem.wait()
    z_end(0)
    y_far(0)
    y_far(1)
    z_step(1, 4)
    z_step(2, 2)
    y_near(0)
    y_far(3)
    z_end(1)
    y_far(2)
    y_near(1)
    y_far(4)
    z_step(2, 3)
    w_last()
    y_near(2)
    y_end(0)
    attention(1)
    z_step(2, 4)
    y_near(3)
    z_end(2)
    y_far(5)
    y_near(4)
    x_pass(1)
    y_end(1)
    y_end(2)
    attention(2)
    y_near(5)
    in_r.wait()
    w_end()
    x_end(0)
    project(0)
    x_pass(2)
    x_end(1)
    project(1)
    y_end(3)
    y_end(4)
    y_end(5)
    attention(3)
    family()
    x_end(2)
    project(2)
    x_pass(3)
    x_end(3)
    project(3)
    tail()
    for copy in out_copies:
        copy.wait()
    for copy in started:
        copy.wait_send()


def body(queries, keys, values, resid, out_weight, norm_gain, value_weight, parent, counts):
    leaf = lax.axis_index("leaf")
    row = lax.broadcasted_iota(jnp.int32, (8, 128), 0)
    wide = jnp.pad(parent, (0, 128 - SLOTS))[None, :]
    ptile = jnp.where(row == lax.rem(leaf, 8), wide, 0)
    dma = pltpu.SemaphoreType.DMA
    vm = pltpu.VMEM
    scratch = [
        vm((SLOTS, BLK, COLS), BF16),
        vm((SLOTS, BLK, DH), BF16),
        vm((SLOTS, BLK, DH), BF16),
        vm((SLOTS, BLK, WIDTH), BF16),
        vm((4, COLS, WIDTH), BF16),
        vm((ZC, 2, W, BLK, DH), BF16),
        vm((ZC, 2, W, BLK, DH), BF16),
        vm((ZC, 2, W, BLK, DH), BF16),
        vm((4, LEVELS, ROWS, COLS), BF16),
        vm((6, W, 2, BLK, DH), BF16),
        vm((6, W, 2, BLK, DH), BF16),
        vm((6, W, 2, BLK, DH), BF16),
        vm((6, 2, HALF, 2, BLK, DH), BF16),
        vm((6, 2, W, 2, BLK, DH), BF16),
        vm((SLOTS, BLK, WIDTH), BF16),
        vm((ZC, 8, 128), jnp.int32),
        vm((NY, 2, 8, 128), jnp.int32),
        vm((ZC, 8, 128), F32),
        vm((NY, 2, 8, 128), F32),
        pltpu.SMEM((NY * ZC, 128), jnp.int32),
        vm((128, 128), jnp.int32),
        vm((3, 64, W * 128), BF16),
        vm((3, W * 128, 128), F32),
        vm((3, 64, 128), F32),
        vm((3, 64, 128), F32),
        vm((16, 128), F32),
        vm((3, 16, 128), F32),
        vm((8, 128), F32),
        vm((ROWS, 128), F32),
        vm((ROWS, 128), F32),
        dma((24,)),
        dma((3, 2, 4)), dma((3, 2, 4)),
        dma((3, 8)), dma((3, 8)),
        dma((6, 2)), dma((6, 2)),
        dma((6, 2)), dma((6, 2)),
        dma((4, 4)), dma((4, 4)),
        dma((3,)), dma((3,)),
        dma((4,)), dma((4,)),
        dma((4,)), dma((4,)),
        dma((2, ZC)), dma((2, ZC)),
        dma((2, 3)), dma((2, 3)),
        dma((3,)), dma((3,)),
    ]
    hbm = pl.BlockSpec(memory_space=pl.ANY)
    whole = pl.BlockSpec(memory_space=pltpu.VMEM)
    hidden, backed = pl.pallas_call(
        kernel,
        out_shape=(
            jax.ShapeDtypeStruct((SLOTS, BLK, WIDTH), BF16),
            jax.ShapeDtypeStruct((1, 128), F32),
        ),
        in_specs=[hbm, hbm, hbm, hbm, hbm, whole, whole, whole, pl.BlockSpec(memory_space=pltpu.SMEM)],
        out_specs=(hbm, whole),
        scratch_shapes=scratch,
        compiler_params=pltpu.CompilerParams(
            collective_id=0, has_side_effects=True, vmem_limit_bytes=56 * 1024 * 1024
        ),
    )(
        queries, keys, values, resid, out_weight,
        norm_gain.reshape(1, WIDTH), value_weight.reshape(1, WIDTH), ptile, counts,
    )
    alive = jnp.arange(SLOTS, dtype=jnp.int32) < counts[0]
    layer_out = jnp.where(alive[:, None, None], hidden, jnp.zeros_like(hidden))
    return (layer_out, backed[0, :SLOTS])


def solution(mesh):
    in_specs = (
        P("leaf", None, "tensor"),
        P("leaf", None, "tensor"),
        P("leaf", None, "tensor"),
        P("leaf", None, "tensor"),
        P("tensor", None),
        P("tensor"),
        P("tensor"),
        P("leaf"),
        P("leaf"),
    )
    out_specs = (P("leaf", None, "tensor"), P("leaf"))
    return jax.shard_map(body, mesh=mesh, in_specs=in_specs, out_specs=out_specs, check_vma=False)
```

```python
import math

import jax
import jax.numpy as jnp
from jax import lax
from jax.experimental import pallas as pl
from jax.experimental.pallas import tpu as pltpu
from jax.sharding import PartitionSpec as P

D = 4096
DH = 128
BLK = 32
LEVELS = 4
W = 8
NX, NY, NZ, NC = 4, 4, 8, 2
ZC = NZ * NC
SLOTS = LEVELS * W
HEADS_HERE = 4
ROWS = W * BLK
COLS = HEADS_HERE * DH
WIDTH = D // NX
WROWS = COLS // (NY * NC)
TILE = 256
HALF = W // 2
BATCHES = ((0, 1), (0, 2), (1, 2), (0, 3), (1, 3), (2, 3))

norm_eps = 1e-05
masked_score = -1e30
BF16 = jnp.bfloat16
F32 = jnp.float32
MESH = pl.DeviceIdType.MESH


def kernel(
    q_hbm, k_hbm, v_hbm, r_hbm, w_hbm, gain_ref, vw_ref, parent_ref, counts_ref,
    hid_v, bk_ref,
    q_v, k_v, v_v, r_v, wf, kvg0, kvg1, kvg2, ag, ysa, ysp, ysm, yh, yr,
    ptl, pyr, pbuf, gr, gyr, psm, pvm, amat, bmat, invm, keepm, stats, srecv, rtile, sqacc, mxacc, mix,
    lsem, zs, zr, sbs, sbr, yas, yar, yfs, yfr, xs, xr, wxs, wxr, wys, wyr, wbs, wbr,
    pys, pyrv, ps, pr, pbs, pbr, gys, gyrv, gs, grv, sts, strv,
):
    kvg = (kvg0, kvg1, kvg2)
    leaf = lax.axis_index("leaf")
    x = lax.axis_index("tensor")
    c = lax.rem(leaf, NC)
    z = lax.rem(leaf // NC, NZ)
    y = leaf // ZC
    zc = lax.rem(leaf, ZC)

    def leaf_of(yy, zz, cc):
        return (yy * NZ + zz) * NC + cc

    def shift(v, d, n):
        return lax.rem(v + d + n, n)

    yp, ym, ya2 = shift(y, 1, NY), shift(y, -1, NY), shift(y, 2, NY)
    xp, xm, xa = shift(x, 1, NX), shift(x, -1, NX), shift(x, 2, NX)
    zp, zm = shift(z, 1, NZ), shift(z, -1, NZ)
    at_zp, at_zm = (leaf_of(y, zp, c), x), (leaf_of(y, zm, c), x)
    at_sib = (leaf_of(y, z, 1 - c), x)
    at_yp, at_ym, at_ya = (leaf_of(yp, z, c), x), (leaf_of(ym, z, c), x), (leaf_of(ya2, z, c), x)
    at_xp, at_xm, at_xa = (leaf, xp), (leaf, xm), (leaf, xa)

    def plane_peer(i):
        return (y * ZC + lax.rem(zc + i, ZC), x)

    started = []

    def remote(src, dst, ssem, rsem, dev):
        copy = pltpu.make_async_remote_copy(
            src_ref=src, dst_ref=dst, send_sem=ssem, recv_sem=rsem, device_id=dev, device_id_type=MESH
        )
        return copy

    def send(src, dst, ssem, rsem, dev):
        copy = remote(src, dst, ssem, rsem, dev)
        copy.start()
        started.append(copy)

    def arrived(ref, ssem, rsem):
        remote(ref, ref, ssem, rsem, at_sib).wait_recv()

    barrier = pltpu.get_barrier_semaphore()
    partners = [at_zp, at_zm, at_sib, at_yp, at_ym, at_ya, at_xp, at_xm, at_xa]
    for dev in partners:
        pl.semaphore_signal(barrier, inc=1, device_id=dev, device_id_type=MESH)

    locals_ = []

    def local(src, dst):
        copy = pltpu.make_async_copy(src, dst, lsem.at[len(locals_)])
        copy.start()
        locals_.append(copy)
        return copy

    own_kv = []
    for l in range(3):
        own_kv.append(
            (
                local(k_hbm.at[pl.ds(W * l, W)], kvg[l].at[zc, 0]),
                local(v_hbm.at[pl.ds(W * l, W)], kvg[l].at[zc, 1]),
            )
        )
    in_q = local(q_hbm, q_v)
    in_k = local(k_hbm, k_v)
    in_v = local(v_hbm, v_v)
    in_w = local(w_hbm.at[:, pl.ds(pl.multiple_of(x * WIDTH, WIDTH), WIDTH)], wf.at[3])
    in_r = local(r_hbm, r_v)
    pl.semaphore_wait(barrier, len(partners))

    sub = lax.broadcasted_iota(jnp.int32, (8, 128), 0)
    ln = lax.broadcasted_iota(jnp.int32, (8, 128), 1)
    mine_sub = sub == c * NY + y
    mine_row = z * 8 + c * NY + y
    y_peers = (at_yp, at_ym, at_ya)

    def p_send():
        row = jnp.zeros((8, 128), jnp.int32)
        for n in range(SLOTS):
            row = jnp.where(ln == n, parent_ref[n], row)
        ptl[...] = jnp.where(mine_sub, row, 0)
        for i, dev in enumerate(y_peers):
            send(ptl, pyr.at[i], pys.at[i], pyrv.at[i], dev)

    def p_start():
        for i in range(3):
            arrived(pyr.at[i], pys.at[i], pyrv.at[i])
        pbuf[c, z] = (ptl[...] + pyr[0]) + (pyr[1] + pyr[2])
        own = pbuf.at[c, z]
        send(own, own, ps.at[0, 0], pr.at[0, 0], at_zp)
        send(own, own, ps.at[1, 0], pr.at[1, 0], at_zm)

    def p_step(s):
        for way, d in ((0, -s), (1, s)):
            if s == 4 and way == 1:
                continue
            one = pbuf.at[c, shift(z, d, NZ)]
            arrived(one, ps.at[way, s - 1], pr.at[way, s - 1])
            if s < 3 or (s == 3 and way == 0):
                send(one, one, ps.at[way, s], pr.at[way, s], at_zm if way else at_zp)
        if s == 4:
            send(pbuf.at[c], pbuf.at[c], pbs, pbr, at_sib)

    def p_end():
        arrived(pbuf.at[1 - c], pbs, pbr)
        parents = (pbuf[0] + pbuf[1]).reshape(64, 128)
        pvm[0:64] = parents
        pvm[64:128] = parents
        return local(pvm.at[pl.ds(0, 64)], psm)

    def zidx(d, cc):
        return shift(z, d, NZ) * NC + cc

    def z_start(l):
        for kv in range(2):
            own_kv[l][kv].wait()
            own = kvg[l].at[zc, kv]
            send(own, own, zs.at[l, 0, 0, kv], zr.at[l, 0, 0, kv], at_zp)
            send(own, own, zs.at[l, 1, 0, kv], zr.at[l, 1, 0, kv], at_zm)
        own = kvg[l].at[zc]
        send(own, own, sbs.at[l, 0], sbr.at[l, 0], at_sib)

    def z_step(l, s):
        for kv in range(2):
            for way, d in ((0, -s), (1, s)):
                if s == 4 and kv != way:
                    continue
                piece = kvg[l].at[zidx(d, c), kv]
                arrived(piece, zs.at[l, way, s - 1, kv], zr.at[l, way, s - 1, kv])
                if s < 3 or (s == 3 and kv == way):
                    send(piece, piece, zs.at[l, way, s, kv], zr.at[l, way, s, kv], at_zm if way else at_zp)
        for way, d in ((0, -s), (1, s)):
            if s == 4 and way == 1:
                continue
            shard = kvg[l].at[zidx(d, c)]
            j = 7 if s == 4 else 1 + way * 3 + s - 1
            send(shard, shard, sbs.at[l, j], sbr.at[l, j], at_sib)

    def z_end(l):
        for j, d in enumerate((0, -1, -2, -3, 1, 2, 3, 4)):
            arrived(kvg[l].at[zidx(d, 1 - c)], sbs.at[l, j], sbr.at[l, j])

    def climb(node, hops):
        for _ in range(hops):
            dev = lax.shift_right_logical(node, 5)
            row = (lax.shift_right_logical(dev, 1) & 7) * 8 + (dev & 1) * NY + lax.shift_right_logical(dev, 4)
            node = jnp.maximum(psm[row, node & 31], 0)
        return node

    def locate(dev, l, n, s):
        node = climb(dev * SLOTS + W * l + n, l - s)
        owner = lax.shift_right_logical(node, 5)
        return lax.shift_right_logical(owner, 4), owner & 15, node & 7

    def y_far(b):
        s, l = BATCHES[b]
        dev = ya2 * ZC + zc

        def pick(n, carry):
            _, src, slot = locate(dev, l, n, s)
            for kv in range(2):
                ysa[b, n, kv] = kvg[s][src, kv, slot]
            return carry

        lax.fori_loop(0, W, pick, 0)
        first, second = ysa.at[b, pl.ds(0, HALF)], ysa.at[b, pl.ds(HALF, HALF)]
        send(first, yh.at[b, 0], yas.at[b, 0], yar.at[b, 0], at_yp)
        send(second, yh.at[b, 1], yas.at[b, 1], yar.at[b, 1], at_ym)

    def y_near(b):
        s, l = BATCHES[b]
        arrived(yh.at[b, 0], yas.at[b, 0], yar.at[b, 0])
        arrived(yh.at[b, 1], yas.at[b, 1], yar.at[b, 1])
        dev_p = yp * ZC + zc
        dev_m = ym * ZC + zc

        def pick(n, carry):
            for half in range(2):
                row = half * HALF + n
                for out, dev, way in ((ysp, dev_p, 0), (ysm, dev_m, 1)):
                    col, src, slot = locate(dev, l, row, s)
                    for kv in range(2):
                        mine = kvg[s][src, kv, slot]
                        if half == way:
                            mine = jnp.where(col == y, mine, yh[b, way, n, kv])
                        out[b, row, kv] = mine
            return carry

        lax.fori_loop(0, HALF, pick, 0)
        send(ysp.at[b], yr.at[b, 0], yfs.at[b, 0], yfr.at[b, 0], at_yp)
        send(ysm.at[b], yr.at[b, 1], yfs.at[b, 1], yfr.at[b, 1], at_ym)

    def y_end(b):
        arrived(yr.at[b, 0], yfs.at[b, 0], yfr.at[b, 0])
        arrived(yr.at[b, 1], yfs.at[b, 1], yfr.at[b, 1])

    row_q = lax.broadcasted_iota(jnp.int32, (HEADS_HERE * BLK, LEVELS * BLK), 0) & (BLK - 1)
    key_j = lax.broadcasted_iota(jnp.int32, (HEADS_HERE * BLK, LEVELS * BLK), 1)

    def attention(l):
        allowed = ((key_j < BLK) & (key_j <= row_q)) | ((key_j >= BLK) & (key_j < BLK * (l + 1)))
        mine_dev = leaf

        def one(n, half):
            node = W * l + n
            q_node = q_v[node]
            q_rows = jnp.concatenate([q_node[:, h * DH : (h + 1) * DH] for h in range(HEADS_HERE)], axis=0)
            parts = [[k_v[node]], [v_v[node]]]
            for k in range(1, l + 1):
                s = l - k
                b = BATCHES.index((s, l))
                col, src, slot = locate(mine_dev, l, n, s)
                here = col == y
                if half == 0:
                    from_p = col == yp
                else:
                    from_p = jnp.logical_not(here | (col == ym))
                for kv in range(2):
                    block = jnp.where(from_p, yr[b, 1, n, kv], yr[b, 0, n, kv])
                    block = jnp.where(here, kvg[s][src, kv, slot], block)
                    parts[kv].append(block)
            for kv in range(2):
                for _ in range(l + 1, LEVELS):
                    parts[kv].append(jnp.zeros((BLK, DH), BF16))
            k_all = jnp.concatenate(parts[0], axis=0)
            v_all = jnp.concatenate(parts[1], axis=0)
            scores = lax.dot_general(
                q_rows, k_all, (((1,), (1,)), ((), ())), preferred_element_type=F32
            ) * DH ** (-0.5)
            scores = jnp.where(allowed, scores, masked_score)
            highest = jnp.max(scores, axis=1, keepdims=True)
            expo = jnp.exp(scores - highest)
            weights = (expo / jnp.sum(expo, axis=1, keepdims=True)).astype(BF16)
            got = jnp.dot(weights, v_all, preferred_element_type=F32).astype(BF16)
            rows = pl.ds(pl.multiple_of(n * BLK, BLK), BLK)
            for h in range(HEADS_HERE):
                ag[3, l, rows, h * DH : (h + 1) * DH] = got[h * BLK : (h + 1) * BLK]

        for half in range(2):

            def pair(i, carry):
                for j in range(2):
                    one(half * HALF + 2 * i + j, half)
                return carry

            lax.fori_loop(0, HALF // 2, pair, 0)
        own = ag.at[3, l]
        send(own, ag.at[0, l], xs.at[l, 0], xr.at[l, 0], at_xp)
        send(own, ag.at[1, l], xs.at[l, 1], xr.at[l, 1], at_xm)

    def x_pass(l):
        top, low = pl.ds(0, ROWS // 2), pl.ds(ROWS // 2, ROWS // 2)
        arrived(ag.at[0, l], xs.at[l, 0], xr.at[l, 0])
        send(ag.at[0, l, top], ag.at[2, l, top], xs.at[l, 2], xr.at[l, 2], at_xp)
        arrived(ag.at[1, l], xs.at[l, 1], xr.at[l, 1])
        send(ag.at[1, l, low], ag.at[2, l, low], xs.at[l, 3], xr.at[l, 3], at_xm)

    def x_end(l):
        arrived(ag.at[2, l, pl.ds(0, ROWS // 2)], xs.at[l, 2], xr.at[l, 2])
        arrived(ag.at[2, l, pl.ds(ROWS // 2, ROWS // 2)], xs.at[l, 3], xr.at[l, 3])

    def w_rows(yy, cc):
        return pl.ds(pl.multiple_of((yy * NC + cc) * WROWS, WROWS), WROWS)

    def w_start():
        rows = w_rows(y, c)
        for slot, to, dev in ((0, xp, at_xp), (1, xm, at_xm), (2, xa, at_xa)):
            cols = pl.ds(pl.multiple_of(to * WIDTH, WIDTH), WIDTH)
            send(w_hbm.at[rows, cols], wf.at[slot, rows], wxs.at[slot], wxr.at[slot], dev)

    three = pl.ds(0, 3)

    def w_mid():
        rows = w_rows(y, c)
        for slot in range(3):
            arrived(wf.at[slot, rows], wxs.at[slot], wxr.at[slot])
        piece = wf.at[three, rows]
        send(piece, piece, wys.at[0], wyr.at[0], at_yp)
        send(piece, piece, wys.at[1], wyr.at[1], at_ym)
        send(piece, piece, wbs.at[0], wbr.at[0], at_sib)

    def w_halves(yy, cc):
        base = (yy * NC + cc) * WROWS
        return (
            pl.ds(pl.multiple_of(base, WROWS // 2), WROWS // 2),
            pl.ds(pl.multiple_of(base + WROWS // 2, WROWS // 2), WROWS // 2),
        )

    def w_pass():
        for j, (yy, dev) in enumerate(((ym, at_yp), (yp, at_ym))):
            piece = wf.at[three, w_rows(yy, c)]
            arrived(piece, wys.at[j], wyr.at[j])
            onward = wf.at[three, w_halves(yy, c)[j]]
            send(onward, onward, wys.at[2 + j], wyr.at[2 + j], dev)
            send(piece, piece, wbs.at[1 + j], wbr.at[1 + j], at_sib)

    def w_last():
        for j in range(2):
            arrived(wf.at[three, w_halves(ya2, c)[j]], wys.at[2 + j], wyr.at[2 + j])
        piece = wf.at[three, w_rows(ya2, c)]
        send(piece, piece, wbs.at[3], wbr.at[3], at_sib)

    def w_end():
        for j, yy in enumerate((y, ym, yp, ya2)):
            arrived(wf.at[three, w_rows(yy, 1 - c)], wbs.at[j], wbr.at[j])
        in_w.wait()

    def project(l):
        sqacc[...] = jnp.zeros_like(sqacc)
        mxacc[...] = jnp.zeros_like(mxacc)

        def tile(j, carry):
            cols = pl.ds(pl.multiple_of(j * TILE, TILE), TILE)
            total = jnp.dot(ag[3, l], wf[3, :, cols], preferred_element_type=F32)
            for slot in range(3):
                total = total + jnp.dot(ag[slot, l], wf[slot, :, cols], preferred_element_type=F32)
            res = r_v[pl.ds(W * l, W), :, cols].reshape(ROWS, TILE)
            hid = (res.astype(F32) + total).astype(BF16)
            node = W * l + lax.broadcasted_iota(jnp.int32, (W, BLK, TILE), 0)
            hid_v[pl.ds(W * l, W), :, cols] = jnp.where(
                node < counts_ref[0], hid.reshape(W, BLK, TILE), jnp.zeros((W, BLK, TILE), BF16)
            )
            hid_f = hid.astype(F32)
            mixer = mix[:, cols]
            square = hid_f * hid_f
            mixed = hid_f * mixer
            sqacc[...] += square[:, :128] + square[:, 128:]
            mxacc[...] += mixed[:, :128] + mixed[:, 128:]
            return carry

        lax.fori_loop(0, WIDTH // TILE, tile, 0)
        for base, acc in ((0, sqacc), (8, mxacc)):
            for half in range(2):
                turned = acc[half * 128 : (half + 1) * 128].T
                stats[base + 2 * l + half : base + 2 * l + half + 1, :] = jnp.sum(turned, axis=0, keepdims=True)

    def family():
        mix[...] = (gain_ref[...].astype(F32) * vw_ref[...].astype(F32)).reshape(1, WIDTH)
        turned = pvm[...].T
        rows = lax.broadcasted_iota(jnp.int32, (64, 128), 0)
        lanes = lax.broadcasted_iota(jnp.int32, (64, 128), 1)
        first = lax.broadcasted_iota(jnp.int32, (1, 128), 1) < 64
        for l in range(3):
            for j in range(W):
                child = W * (l + 1) + j
                slot = pvm[0:64, child : child + 1] & 31
                bmat[l, j * 64 : (j + 1) * 64, :] = jnp.where(jnp.broadcast_to(slot, (64, 128)) == lanes, 1.0, 0.0)
            for j in range(0, W, 2):
                child = W * (l + 1) + j
                node = jnp.where(first, turned[child : child + 1, :], turned[child + 1 : child + 2, :])
                dev = lax.shift_right_arithmetic(node, 5)
                row = (lax.shift_right_arithmetic(dev, 1) & 7) * 8 + (dev & 1) * NY + lax.shift_right_arithmetic(dev, 4)
                row = jnp.where(node < 0, -1, row)
                amat[l, :, j * 64 : (j + 2) * 64] = jnp.where(
                    jnp.broadcast_to(row, (64, 128)) == rows, 1.0, 0.0
                ).astype(BF16)
            count = jnp.dot(amat[l], bmat[l].astype(BF16), preferred_element_type=F32)
            invm[l] = jnp.where(count > 0, 0.5 / jnp.maximum(count, 1.0), 0.0)
            keepm[l] = jnp.where(count > 0, 0.5, 1.0)

    def tail():
        for i, dev in enumerate((at_xp, at_xm, at_xa)):
            send(stats, srecv.at[i], sts.at[i], strv.at[i], dev)
        for i in range(3):
            arrived(srecv.at[i], sts.at[i], strv.at[i])
        total = (stats[...] + srecv[0]) + (srecv[1] + srecv[2])
        score = total[8:16] / jnp.sqrt(total[0:8] / D + norm_eps)
        jj = lax.broadcasted_iota(jnp.int32, (128, 128), 0)
        nn = lax.broadcasted_iota(jnp.int32, (128, 128), 1)
        group = jnp.where((jj // BLK) == (nn & 3), 1.0, 0.0)
        sums = jnp.dot(score, group, preferred_element_type=F32, precision=lax.Precision.HIGHEST)
        per_node = jnp.sum(jnp.where((ln // 4) == sub, sums, 0.0), axis=0, keepdims=True)
        reward = jnp.tanh(per_node / math.sqrt(BLK))
        wide = jnp.broadcast_to(reward, (8, 128))
        rtile[...] = jnp.where(mine_sub & (ln < counts_ref[0]), wide, 0.0)
        for i, dev in enumerate(y_peers):
            send(rtile, gyr.at[i], gys.at[i], gyrv.at[i], dev)
        for i in range(3):
            arrived(gyr.at[i], gys.at[i], gyrv.at[i])
        gr[c, z] = (rtile[...] + gyr[0]) + (gyr[1] + gyr[2])
        for i in range(1, ZC):
            send(gr.at[c, z], gr.at[c, z], gs.at[i], grv.at[i], plane_peer(i))
        for i in range(1, ZC):
            other = lax.rem(zc + ZC - i, ZC)
            arrived(gr.at[lax.rem(other, NC), other // NC], gs.at[i], grv.at[i])
        values = (gr[0] + gr[1]).reshape(64, 128)
        for l in (2, 1, 0):
            spread = jnp.concatenate(
                [
                    bmat[l, j * 64 : (j + 1) * 64, :]
                    * jnp.broadcast_to(values[:, W * (l + 1) + j : W * (l + 1) + j + 1], (64, 128))
                    for j in range(W)
                ],
                axis=0,
            )
            high = spread.astype(BF16)
            low = (spread - high.astype(F32)).astype(BF16)
            summed = jnp.dot(amat[l], high, preferred_element_type=F32)
            summed = summed + jnp.dot(amat[l], low, preferred_element_type=F32)
            values = keepm[l] * values + invm[l] * summed
        who = lax.broadcasted_iota(jnp.int32, (64, 128), 0)
        bk_ref[...] = jnp.sum(jnp.where(who == mine_row, values, 0.0), axis=0, keepdims=True)

    z_start(0)
    p_send()
    w_start()
    in_q.wait()
    in_k.wait()
    in_v.wait()
    attention(0)
    z_step(0, 1)
    p_start()
    w_mid()
    z_step(0, 2)
    p_step(1)
    z_start(1)
    z_step(0, 3)
    p_step(2)
    p_step(3)
    z_step(0, 4)
    p_step(4)
    z_step(1, 1)
    x_pass(0)
    w_pass()
    to_smem = p_end()
    z_end(0)
    to_smem.wait()
    y_far(0)
    y_far(1)
    z_step(1, 2)
    z_start(2)
    y_far(3)
    y_near(0)
    z_step(1, 3)
    y_near(1)
    z_step(1, 4)
    z_step(2, 1)
    y_near(3)
    w_last()
    y_end(0)
    attention(1)
    z_step(2, 2)
    z_end(1)
    y_far(2)
    y_far(4)
    z_step(2, 3)
    y_near(2)
    y_near(4)
    z_step(2, 4)
    x_pass(1)
    y_end(1)
    y_end(2)
    attention(2)
    z_end(2)
    y_far(5)
    family()
    in_r.wait()
    w_end()
    x_end(0)
    project(0)
    y_near(5)
    x_pass(2)
    x_end(1)
    project(1)
    y_end(3)
    y_end(4)
    y_end(5)
    attention(3)
    x_end(2)
    project(2)
    x_pass(3)
    x_end(3)
    project(3)
    tail()
    for copy in started:
        copy.wait_send()


def body(queries, keys, values, resid, out_weight, norm_gain, value_weight, parent, counts):
    dma = pltpu.SemaphoreType.DMA
    vm = pltpu.VMEM
    scratch = [
        vm((SLOTS, BLK, COLS), BF16),
        vm((SLOTS, BLK, DH), BF16),
        vm((SLOTS, BLK, DH), BF16),
        vm((SLOTS, BLK, WIDTH), BF16),
        vm((4, COLS, WIDTH), BF16),
        vm((ZC, 2, W, BLK, DH), BF16),
        vm((ZC, 2, W, BLK, DH), BF16),
        vm((ZC, 2, W, BLK, DH), BF16),
        vm((4, LEVELS, ROWS, COLS), BF16),
        vm((6, W, 2, BLK, DH), BF16),
        vm((6, W, 2, BLK, DH), BF16),
        vm((6, W, 2, BLK, DH), BF16),
        vm((6, 2, HALF, 2, BLK, DH), BF16),
        vm((6, 2, W, 2, BLK, DH), BF16),
        vm((8, 128), jnp.int32),
        vm((3, 8, 128), jnp.int32),
        vm((NC, NZ, 8, 128), jnp.int32),
        vm((NC, NZ, 8, 128), F32),
        vm((3, 8, 128), F32),
        pltpu.SMEM((64, 128), jnp.int32),
        vm((128, 128), jnp.int32),
        vm((3, 64, W * 64), BF16),
        vm((3, W * 64, 128), F32),
        vm((3, 64, 128), F32),
        vm((3, 64, 128), F32),
        vm((16, 128), F32),
        vm((3, 16, 128), F32),
        vm((8, 128), F32),
        vm((ROWS, 128), F32),
        vm((ROWS, 128), F32),
        vm((1, WIDTH), F32),
        dma((24,)),
        dma((3, 2, 4, 2)), dma((3, 2, 4, 2)),
        dma((3, 8)), dma((3, 8)),
        dma((6, 2)), dma((6, 2)),
        dma((6, 2)), dma((6, 2)),
        dma((4, 4)), dma((4, 4)),
        dma((3,)), dma((3,)),
        dma((4,)), dma((4,)),
        dma((4,)), dma((4,)),
        dma((3,)), dma((3,)),
        dma((2, 4)), dma((2, 4)),
        dma(()), dma(()),
        dma((3,)), dma((3,)),
        dma((ZC,)), dma((ZC,)),
        dma((3,)), dma((3,)),
    ]
    hbm = pl.BlockSpec(memory_space=pl.ANY)
    whole = pl.BlockSpec(memory_space=pltpu.VMEM)
    smem = pl.BlockSpec(memory_space=pltpu.SMEM)
    hidden, backed = pl.pallas_call(
        kernel,
        out_shape=(
            pltpu.VMEM((SLOTS, BLK, WIDTH), BF16),
            pltpu.VMEM((1, 128), F32),
        ),
        in_specs=[hbm, hbm, hbm, hbm, hbm, whole, whole, smem, smem],
        out_specs=(whole, whole),
        scratch_shapes=scratch,
        compiler_params=pltpu.CompilerParams(
            collective_id=0, has_side_effects=True, vmem_limit_bytes=56 * 1024 * 1024
        ),
    )(
        queries, keys, values, resid, out_weight,
        norm_gain, value_weight, parent, counts,
    )
    return (hidden, backed[0, :SLOTS])


def solution(mesh):
    in_specs = (
        P("leaf", None, "tensor"),
        P("leaf", None, "tensor"),
        P("leaf", None, "tensor"),
        P("leaf", None, "tensor"),
        P("tensor", None),
        P("tensor"),
        P("tensor"),
        P("leaf"),
        P("leaf"),
    )
    out_specs = (P("leaf", None, "tensor"), P("leaf"))
    return jax.shard_map(body, mesh=mesh, in_specs=in_specs, out_specs=out_specs, check_vma=False)
```

```python
import math

import jax
import jax.numpy as jnp
from jax import lax
from jax.experimental import pallas as pl
from jax.experimental.pallas import tpu as pltpu
from jax.sharding import PartitionSpec as P

D = 4096
DH = 128
BLK = 32
LEVELS = 4
W = 8
NX, NY, NZ, NC = 4, 4, 8, 2
ZC = NZ * NC
SLOTS = LEVELS * W
HEADS_HERE = 4
ROWS = W * BLK
COLS = HEADS_HERE * DH
WIDTH = D // NX
WROWS = COLS // (NY * NC)
TILE = 256
HALF = W // 2
GROUP = 4
BATCHES = ((0, 1), (0, 2), (1, 2), (0, 3), (1, 3), (2, 3))

norm_eps = 1e-05
masked_score = -1e30
BF16 = jnp.bfloat16
F32 = jnp.float32
MESH = pl.DeviceIdType.MESH


def kernel(
    q_hbm, k_hbm, v_hbm, r_hbm, w_hbm, gain_ref, vw_ref, parent_ref, counts_ref,
    hid_v, bk_ref,
    q_v, k_v, v_v, r_v, wf, kvg0, kvg1, kvg2, ag, ysa, ysp, ysm, yh, yr,
    ptl, pyr, pbuf, gr, gyr, psm, pvm, amat, bmat, invm, keepm, stats, srecv, rtile, sqacc, mxacc, mix, partial,
    lsem, zs, zr, sbs, sbr, yas, yar, yfs, yfr, xs, xr, wxs, wxr, wys, wyr, wbs, wbr,
    pys, pyrv, ps, pr, pbs, pbr, gys, gyrv, gs, grv, sts, strv,
):
    kvg = (kvg0, kvg1, kvg2)
    leaf = lax.axis_index("leaf")
    x = lax.axis_index("tensor")
    c = lax.rem(leaf, NC)
    z = lax.rem(leaf // NC, NZ)
    y = leaf // ZC
    zc = lax.rem(leaf, ZC)

    def leaf_of(yy, zz, cc):
        return (yy * NZ + zz) * NC + cc

    def shift(v, d, n):
        return lax.rem(v + d + n, n)

    yp, ym, ya2 = shift(y, 1, NY), shift(y, -1, NY), shift(y, 2, NY)
    xp, xm, xa = shift(x, 1, NX), shift(x, -1, NX), shift(x, 2, NX)
    zp, zm = shift(z, 1, NZ), shift(z, -1, NZ)
    at_zp, at_zm = (leaf_of(y, zp, c), x), (leaf_of(y, zm, c), x)
    at_sib = (leaf_of(y, z, 1 - c), x)
    at_yp, at_ym, at_ya = (leaf_of(yp, z, c), x), (leaf_of(ym, z, c), x), (leaf_of(ya2, z, c), x)
    at_xp, at_xm, at_xa = (leaf, xp), (leaf, xm), (leaf, xa)

    started = []

    def remote(src, dst, ssem, rsem, dev):
        copy = pltpu.make_async_remote_copy(
            src_ref=src, dst_ref=dst, send_sem=ssem, recv_sem=rsem, device_id=dev, device_id_type=MESH
        )
        return copy

    def send(src, dst, ssem, rsem, dev):
        copy = remote(src, dst, ssem, rsem, dev)
        copy.start()
        started.append(copy)

    def drain():
        for copy in started:
            copy.wait_send()
        started.clear()

    def drain_some(keep):
        while len(started) > keep:
            started.pop(0).wait_send()

    def arrived(ref, ssem, rsem):
        remote(ref, ref, ssem, rsem, at_sib).wait_recv()

    barrier = pltpu.get_barrier_semaphore()
    partners = [at_zp, at_zm, at_sib, at_yp, at_ym, at_ya, at_xp, at_xm, at_xa]
    for dev in partners:
        pl.semaphore_signal(barrier, inc=1, device_id=dev, device_id_type=MESH)

    locals_ = []

    def local(src, dst):
        copy = pltpu.make_async_copy(src, dst, lsem.at[len(locals_)])
        copy.start()
        locals_.append(copy)
        return copy

    own_kv = []
    for l in range(3):
        own_kv.append(
            (
                local(k_hbm.at[pl.ds(W * l, W)], kvg[l].at[zc, 0]),
                local(v_hbm.at[pl.ds(W * l, W)], kvg[l].at[zc, 1]),
            )
        )
    in_q = local(q_hbm, q_v)
    in_k = local(k_hbm, k_v)
    in_v = local(v_hbm, v_v)
    in_w = local(w_hbm.at[:, pl.ds(pl.multiple_of(x * WIDTH, WIDTH), WIDTH)], wf.at[3])
    in_r = local(r_hbm, r_v)
    pl.semaphore_wait(barrier, len(partners))

    sub = lax.broadcasted_iota(jnp.int32, (8, 128), 0)
    ln = lax.broadcasted_iota(jnp.int32, (8, 128), 1)
    mine_sub = sub == c * NY + y
    mine_row = z * 8 + c * NY + y
    y_peers = (at_yp, at_ym, at_ya)

    def p_send():
        row = jnp.zeros((8, 128), jnp.int32)
        for n in range(SLOTS):
            row = jnp.where(ln == n, parent_ref[n], row)
        ptl[...] = jnp.where(mine_sub, row, 0)
        for i, dev in enumerate(y_peers):
            send(ptl, pyr.at[i], pys.at[i], pyrv.at[i], dev)

    def p_start():
        for i in range(3):
            arrived(pyr.at[i], pys.at[i], pyrv.at[i])
        pbuf[c, z] = (ptl[...] + pyr[0]) + (pyr[1] + pyr[2])
        own = pbuf.at[c, z]
        send(own, own, ps.at[0, 0], pr.at[0, 0], at_zp)
        send(own, own, ps.at[1, 0], pr.at[1, 0], at_zm)

    def p_step(s):
        for way, d in ((0, -s), (1, s)):
            one = pbuf.at[c, shift(z, d, NZ)]
            arrived(one, ps.at[way, s - 1], pr.at[way, s - 1])
            if s < 3:
                send(one, one, ps.at[way, s], pr.at[way, s], at_zm if way else at_zp)
            if s == 2 and way == 0:
                send(one, one, ps.at[0, 3], pr.at[0, 3], (leaf_of(y, shift(z, 2, NZ), c), x))
        if s == 3:
            arrived(pbuf.at[c, shift(z, 4, NZ)], ps.at[0, 3], pr.at[0, 3])
            send(pbuf.at[c], pbuf.at[c], pbs, pbr, at_sib)

    def p_end():
        arrived(pbuf.at[1 - c], pbs, pbr)
        parents = (pbuf[0] + pbuf[1]).reshape(64, 128)
        pvm[0:64] = parents
        pvm[64:128] = parents
        return local(pvm.at[pl.ds(0, 64)], psm)

    def zidx(d, cc):
        return shift(z, d, NZ) * NC + cc

    def z_start(l, kv):
        own_kv[l][kv].wait()
        own = kvg[l].at[zc, kv]
        send(own, own, zs.at[l, 0, 0, kv], zr.at[l, 0, 0, kv], at_zp)
        send(own, own, zs.at[l, 1, 0, kv], zr.at[l, 1, 0, kv], at_zm)
        if kv == 1:
            own = kvg[l].at[zc]
            send(own, own, sbs.at[l, 0], sbr.at[l, 0], at_sib)

    def z_step(l, kv, s):
        for way, d in ((0, -s), (1, s)):
            if s == 4 and kv != way:
                continue
            shard = kvg[l].at[zidx(d, c)]
            piece = shard.at[kv]
            arrived(piece, zs.at[l, way, s - 1, kv], zr.at[l, way, s - 1, kv])
            if s < 3 or (s == 3 and kv == way):
                send(piece, piece, zs.at[l, way, s, kv], zr.at[l, way, s, kv], at_zm if way else at_zp)
            if kv == 1:
                j = 7 if s == 4 else 1 + way * 3 + s - 1
                send(shard, shard, sbs.at[l, j], sbr.at[l, j], at_sib)

    def z_end(l):
        for j, d in enumerate((0, -1, -2, -3, 1, 2, 3, 4)):
            arrived(kvg[l].at[zidx(d, 1 - c)], sbs.at[l, j], sbr.at[l, j])

    def climb(node, hops):
        for _ in range(hops):
            dev = lax.shift_right_logical(node, 5)
            row = (lax.shift_right_logical(dev, 1) & 7) * 8 + (dev & 1) * NY + lax.shift_right_logical(dev, 4)
            node = jnp.maximum(psm[row, node & 31], 0)
        return node

    def locate(dev, l, n, s):
        node = climb(dev * SLOTS + W * l + n, l - s)
        owner = lax.shift_right_logical(node, 5)
        return lax.shift_right_logical(owner, 4), owner & 15, node & 7

    def y_far(b):
        s, l = BATCHES[b]
        dev = ya2 * ZC + zc

        def pick(n, carry):
            _, src, slot = locate(dev, l, n, s)
            for kv in range(2):
                ysa[b, n, kv] = kvg[s][src, kv, slot]
            return carry

        lax.fori_loop(0, W, pick, 0)
        first, second = ysa.at[b, pl.ds(0, HALF)], ysa.at[b, pl.ds(HALF, HALF)]
        send(first, yh.at[b, 0], yas.at[b, 0], yar.at[b, 0], at_yp)
        send(second, yh.at[b, 1], yas.at[b, 1], yar.at[b, 1], at_ym)

    def y_near(b):
        s, l = BATCHES[b]
        dev_p = yp * ZC + zc
        dev_m = ym * ZC + zc
        for half in range(2):
            arrived(yh.at[b, half], yas.at[b, half], yar.at[b, half])

            def pick(n, carry):
                row = half * HALF + n
                for out, dev, way in ((ysp, dev_p, 0), (ysm, dev_m, 1)):
                    col, src, slot = locate(dev, l, row, s)
                    for kv in range(2):
                        mine = kvg[s][src, kv, slot]
                        if half == way:
                            mine = jnp.where(col == y, mine, yh[b, way, n, kv])
                        out[b, row, kv] = mine
                return carry

            lax.fori_loop(0, HALF, pick, 0)
            rows = pl.ds(half * HALF, HALF)
            send(ysp.at[b, rows], yr.at[b, 0, rows], yfs.at[b, 0, half], yfr.at[b, 0, half], at_yp)
            send(ysm.at[b, rows], yr.at[b, 1, rows], yfs.at[b, 1, half], yfr.at[b, 1, half], at_ym)

    def y_end(b, half):
        rows = pl.ds(half * HALF, HALF)
        for way in range(2):
            arrived(yr.at[b, way, rows], yfs.at[b, way, half], yfr.at[b, way, half])

    row_q = lax.broadcasted_iota(jnp.int32, (HEADS_HERE * BLK, LEVELS * BLK), 0) & (BLK - 1)
    key_j = lax.broadcasted_iota(jnp.int32, (HEADS_HERE * BLK, LEVELS * BLK), 1)

    def attention(l):
        allowed = ((key_j < BLK) & (key_j <= row_q)) | ((key_j >= BLK) & (key_j < BLK * (l + 1)))
        mine_dev = leaf

        def load(n, half):
            node = W * l + n
            q_node = q_v[node]
            q_rows = jnp.concatenate([q_node[:, h * DH : (h + 1) * DH] for h in range(HEADS_HERE)], axis=0)
            parts = [[k_v[node]], [v_v[node]]]
            for k in range(1, l + 1):
                s = l - k
                b = BATCHES.index((s, l))
                col, src, slot = locate(mine_dev, l, n, s)
                here = col == y
                if half == 0:
                    from_p = col == yp
                else:
                    from_p = jnp.logical_not(here | (col == ym))
                for kv in range(2):
                    block = jnp.where(from_p, yr[b, 1, n, kv], yr[b, 0, n, kv])
                    block = jnp.where(here, kvg[s][src, kv, slot], block)
                    parts[kv].append(block)
            for kv in range(2):
                for _ in range(l + 1, LEVELS):
                    parts[kv].append(jnp.zeros((BLK, DH), BF16))
            return q_rows, jnp.concatenate(parts[0], axis=0), jnp.concatenate(parts[1], axis=0)

        def weigh(scores):
            scores = jnp.where(allowed, scores * DH ** (-0.5), masked_score)
            highest = jnp.max(scores, axis=1, keepdims=True)
            expo = jnp.exp(scores - highest)
            return (expo / jnp.sum(expo, axis=1, keepdims=True)).astype(BF16)

        for half in range(2):
            for s in range(l):
                y_end(BATCHES.index((s, l)), half)

            def group(i, carry):
                first = half * HALF + i * GROUP
                loaded = [load(first + j, half) for j in range(GROUP)]
                scores = [
                    lax.dot_general(q, k, (((1,), (1,)), ((), ())), preferred_element_type=F32) for q, k, _ in loaded
                ]
                weights = [weigh(one) for one in scores]
                for j in range(GROUP):
                    got = jnp.dot(weights[j], loaded[j][2], preferred_element_type=F32).astype(BF16)
                    rows = pl.ds(pl.multiple_of((first + j) * BLK, BLK), BLK)
                    for h in range(HEADS_HERE):
                        ag[3, l, rows, h * DH : (h + 1) * DH] = got[h * BLK : (h + 1) * BLK]
                return carry

            lax.fori_loop(0, HALF // GROUP, group, 0)
            rows = pl.ds(half * HALF * BLK, HALF * BLK)
            own = ag.at[3, l, rows]
            send(own, ag.at[0, l, rows], xs.at[l, half, 0], xr.at[l, half, 0], at_xp)
            send(own, ag.at[1, l, rows], xs.at[l, half, 1], xr.at[l, half, 1], at_xm)

    def x_parts(half):
        quarter = HALF * BLK // 2
        return pl.ds(half * 2 * quarter, quarter), pl.ds(half * 2 * quarter + quarter, quarter)

    def x_pass(l, half):
        rows = pl.ds(half * HALF * BLK, HALF * BLK)
        top, low = x_parts(half)
        arrived(ag.at[0, l, rows], xs.at[l, half, 0], xr.at[l, half, 0])
        send(ag.at[0, l, top], ag.at[2, l, top], xs.at[l, half, 2], xr.at[l, half, 2], at_xp)
        arrived(ag.at[1, l, rows], xs.at[l, half, 1], xr.at[l, half, 1])
        send(ag.at[1, l, low], ag.at[2, l, low], xs.at[l, half, 3], xr.at[l, half, 3], at_xm)

    def x_end(l):
        for half in range(2):
            for way, part in enumerate(x_parts(half)):
                arrived(ag.at[2, l, part], xs.at[l, half, 2 + way], xr.at[l, half, 2 + way])

    def w_rows(yy, cc):
        return pl.ds(pl.multiple_of((yy * NC + cc) * WROWS, WROWS), WROWS)

    def w_start():
        rows = w_rows(y, c)
        for slot, to, dev in ((0, xp, at_xp), (1, xm, at_xm), (2, xa, at_xa)):
            cols = pl.ds(pl.multiple_of(to * WIDTH, WIDTH), WIDTH)
            send(w_hbm.at[rows, cols], wf.at[slot, rows], wxs.at[slot], wxr.at[slot], dev)

    three = pl.ds(0, 3)

    def w_mid():
        rows = w_rows(y, c)
        for slot in range(3):
            arrived(wf.at[slot, rows], wxs.at[slot], wxr.at[slot])
        piece = wf.at[three, rows]
        send(piece, piece, wys.at[0], wyr.at[0], at_yp)
        send(piece, piece, wys.at[1], wyr.at[1], at_ym)
        send(piece, piece, wbs.at[0], wbr.at[0], at_sib)

    def w_halves(yy, cc):
        base = (yy * NC + cc) * WROWS
        return (
            pl.ds(pl.multiple_of(base, WROWS // 2), WROWS // 2),
            pl.ds(pl.multiple_of(base + WROWS // 2, WROWS // 2), WROWS // 2),
        )

    def w_pass():
        for j, (yy, dev) in enumerate(((ym, at_yp), (yp, at_ym))):
            piece = wf.at[three, w_rows(yy, c)]
            arrived(piece, wys.at[j], wyr.at[j])
            onward = wf.at[three, w_halves(yy, c)[j]]
            send(onward, onward, wys.at[2 + j], wyr.at[2 + j], dev)
            send(piece, piece, wbs.at[1 + j], wbr.at[1 + j], at_sib)

    def w_last():
        for j in range(2):
            arrived(wf.at[three, w_halves(ya2, c)[j]], wys.at[2 + j], wyr.at[2 + j])
        piece = wf.at[three, w_rows(ya2, c)]
        send(piece, piece, wbs.at[3], wbr.at[3], at_sib)

    def w_end():
        for j, yy in enumerate((y, ym, yp, ya2)):
            arrived(wf.at[three, w_rows(yy, 1 - c)], wbs.at[j], wbr.at[j])
        in_w.wait()

    def project_near(l):
        def tile(j, carry):
            cols = pl.ds(pl.multiple_of(j * TILE, TILE), TILE)
            total = r_v[pl.ds(W * l, W), :, cols].reshape(ROWS, TILE).astype(F32)
            for slot in (3, 0, 1):
                total = total + jnp.dot(ag[slot, l], wf[slot, :, cols], preferred_element_type=F32)
            partial[:, cols] = total
            return carry

        lax.fori_loop(0, WIDTH // TILE, tile, 0)

    def project_far(l):
        sqacc[...] = jnp.zeros_like(sqacc)
        mxacc[...] = jnp.zeros_like(mxacc)

        def tile(j, carry):
            cols = pl.ds(pl.multiple_of(j * TILE, TILE), TILE)
            total = partial[:, cols] + jnp.dot(ag[2, l], wf[2, :, cols], preferred_element_type=F32)
            hid = total.astype(BF16)
            node = W * l + lax.broadcasted_iota(jnp.int32, (W, BLK, TILE), 0)
            hid_v[pl.ds(W * l, W), :, cols] = jnp.where(
                node < counts_ref[0], hid.reshape(W, BLK, TILE), jnp.zeros((W, BLK, TILE), BF16)
            )
            hid_f = hid.astype(F32)
            square = hid_f * hid_f
            mixed = hid_f * mix[:, cols]
            sqacc[...] += square[:, :128] + square[:, 128:]
            mxacc[...] += mixed[:, :128] + mixed[:, 128:]
            return carry

        lax.fori_loop(0, WIDTH // TILE, tile, 0)
        for base, acc in ((0, sqacc), (8, mxacc)):
            for half in range(2):
                turned = acc[half * 128 : (half + 1) * 128].T
                stats[base + 2 * l + half : base + 2 * l + half + 1, :] = jnp.sum(turned, axis=0, keepdims=True)

    def family():
        mix[...] = (gain_ref[...].astype(F32) * vw_ref[...].astype(F32)).reshape(1, WIDTH)
        turned = pvm[...].T
        rows = lax.broadcasted_iota(jnp.int32, (64, 128), 0)
        lanes = lax.broadcasted_iota(jnp.int32, (64, 128), 1)
        first = lax.broadcasted_iota(jnp.int32, (1, 128), 1) < 64
        for l in range(3):
            for j in range(W):
                child = W * (l + 1) + j
                slot = pvm[0:64, child : child + 1] & 31
                bmat[l, j * 64 : (j + 1) * 64, :] = jnp.where(jnp.broadcast_to(slot, (64, 128)) == lanes, 1.0, 0.0)
            for j in range(0, W, 2):
                child = W * (l + 1) + j
                node = jnp.where(first, turned[child : child + 1, :], turned[child + 1 : child + 2, :])
                dev = lax.shift_right_arithmetic(node, 5)
                row = (lax.shift_right_arithmetic(dev, 1) & 7) * 8 + (dev & 1) * NY + lax.shift_right_arithmetic(dev, 4)
                row = jnp.where(node < 0, -1, row)
                amat[l, :, j * 64 : (j + 2) * 64] = jnp.where(
                    jnp.broadcast_to(row, (64, 128)) == rows, 1.0, 0.0
                ).astype(BF16)
            count = jnp.dot(amat[l], bmat[l].astype(BF16), preferred_element_type=F32)
            invm[l] = jnp.where(count > 0, 0.5 / jnp.maximum(count, 1.0), 0.0)
            keepm[l] = jnp.where(count > 0, 0.5, 1.0)

    def tail():
        for i, dev in enumerate((at_xp, at_xm, at_xa)):
            send(stats, srecv.at[i], sts.at[i], strv.at[i], dev)
        drain()
        for i in range(3):
            arrived(srecv.at[i], sts.at[i], strv.at[i])
        total = (stats[...] + srecv[0]) + (srecv[1] + srecv[2])
        score = total[8:16] / jnp.sqrt(total[0:8] / D + norm_eps)
        jj = lax.broadcasted_iota(jnp.int32, (128, 128), 0)
        nn = lax.broadcasted_iota(jnp.int32, (128, 128), 1)
        group = jnp.where((jj // BLK) == (nn & 3), 1.0, 0.0)
        sums = jnp.dot(score, group, preferred_element_type=F32, precision=lax.Precision.HIGHEST)
        per_node = jnp.sum(jnp.where((ln // 4) == sub, sums, 0.0), axis=0, keepdims=True)
        reward = jnp.tanh(per_node / math.sqrt(BLK))
        wide = jnp.broadcast_to(reward, (8, 128))
        rtile[...] = jnp.where(mine_sub & (ln < counts_ref[0]), wide, 0.0)
        for i in range(1, 8):
            yy, cc = shift(y, i // 2, NY), c if i % 2 == 0 else 1 - c
            send(rtile, gyr.at[i], gys.at[i], gyrv.at[i], (leaf_of(yy, z, cc), x))
        for i in range(1, 8):
            arrived(gyr.at[i], gys.at[i], gyrv.at[i])
        merged = rtile[...]
        for i in range(1, 8):
            merged = merged + gyr[i]
        gr[z] = merged
        for i in range(1, NZ):
            send(gr.at[z], gr.at[z], gs.at[i], grv.at[i], (leaf_of(y, shift(z, i, NZ), c), x))
        drain_some(7)
        for i in range(1, NZ):
            arrived(gr.at[shift(z, -i, NZ)], gs.at[i], grv.at[i])
        values = gr[...].reshape(64, 128)
        for l in (2, 1, 0):
            spread = jnp.concatenate(
                [
                    bmat[l, j * 64 : (j + 1) * 64, :]
                    * jnp.broadcast_to(values[:, W * (l + 1) + j : W * (l + 1) + j + 1], (64, 128))
                    for j in range(W)
                ],
                axis=0,
            )
            high = spread.astype(BF16)
            low = (spread - high.astype(F32)).astype(BF16)
            summed = jnp.dot(amat[l], high, preferred_element_type=F32)
            summed = summed + jnp.dot(amat[l], low, preferred_element_type=F32)
            values = keepm[l] * values + invm[l] * summed
        who = lax.broadcasted_iota(jnp.int32, (64, 128), 0)
        bk_ref[...] = jnp.sum(jnp.where(who == mine_row, values, 0.0), axis=0, keepdims=True)

    p_send()
    z_start(0, 0)
    z_start(0, 1)
    z_start(1, 0)
    w_start()
    p_start()
    z_step(0, 0, 1)
    z_step(0, 1, 1)
    p_step(1)
    z_step(1, 0, 1)
    z_start(1, 1)
    in_q.wait()
    in_k.wait()
    in_v.wait()
    attention(0)
    w_mid()
    p_step(2)
    z_step(0, 0, 2)
    z_step(0, 1, 2)
    z_step(1, 0, 2)
    z_step(1, 1, 1)
    p_step(3)
    z_step(0, 0, 3)
    z_step(0, 1, 3)
    z_step(1, 0, 3)
    z_step(1, 1, 2)
    z_start(2, 0)
    z_start(2, 1)
    to_smem = p_end()
    x_pass(0, 0)
    x_pass(0, 1)
    z_step(0, 0, 4)
    z_step(0, 1, 4)
    w_pass()
    z_end(0)
    to_smem.wait()
    y_far(0)
    y_far(1)
    z_step(1, 0, 4)
    z_step(1, 1, 3)
    z_step(2, 0, 1)
    z_step(2, 1, 1)
    y_far(3)
    z_step(1, 1, 4)
    y_near(0)
    z_end(1)
    z_step(2, 0, 2)
    z_step(2, 1, 2)
    y_far(2)
    y_near(1)
    y_far(4)
    z_step(2, 0, 3)
    z_step(2, 1, 3)
    w_last()
    y_near(2)
    attention(1)
    z_step(2, 0, 4)
    z_step(2, 1, 4)
    y_near(3)
    z_end(2)
    y_far(5)
    y_near(4)
    attention(2)
    x_pass(1, 0)
    x_pass(1, 1)
    y_near(5)
    x_pass(2, 0)
    x_pass(2, 1)
    attention(3)
    family()
    in_r.wait()
    w_end()
    project_near(0)
    x_end(0)
    project_far(0)
    x_pass(3, 0)
    project_near(1)
    x_end(1)
    project_far(1)
    project_near(2)
    x_end(2)
    project_far(2)
    x_pass(3, 1)
    project_near(3)
    x_end(3)
    project_far(3)
    tail()
    drain()


def body(queries, keys, values, resid, out_weight, norm_gain, value_weight, parent, counts):
    dma = pltpu.SemaphoreType.DMA
    vm = pltpu.VMEM
    scratch = [
        vm((SLOTS, BLK, COLS), BF16),
        vm((SLOTS, BLK, DH), BF16),
        vm((SLOTS, BLK, DH), BF16),
        vm((SLOTS, BLK, WIDTH), BF16),
        vm((4, COLS, WIDTH), BF16),
        vm((ZC, 2, W, BLK, DH), BF16),
        vm((ZC, 2, W, BLK, DH), BF16),
        vm((ZC, 2, W, BLK, DH), BF16),
        vm((4, LEVELS, ROWS, COLS), BF16),
        vm((6, W, 2, BLK, DH), BF16),
        vm((6, W, 2, BLK, DH), BF16),
        vm((6, W, 2, BLK, DH), BF16),
        vm((6, 2, HALF, 2, BLK, DH), BF16),
        vm((6, 2, W, 2, BLK, DH), BF16),
        vm((8, 128), jnp.int32),
        vm((3, 8, 128), jnp.int32),
        vm((NC, NZ, 8, 128), jnp.int32),
        vm((NZ, 8, 128), F32),
        vm((8, 8, 128), F32),
        pltpu.SMEM((64, 128), jnp.int32),
        vm((128, 128), jnp.int32),
        vm((3, 64, W * 64), BF16),
        vm((3, W * 64, 128), F32),
        vm((3, 64, 128), F32),
        vm((3, 64, 128), F32),
        vm((16, 128), F32),
        vm((3, 16, 128), F32),
        vm((8, 128), F32),
        vm((ROWS, 128), F32),
        vm((ROWS, 128), F32),
        vm((1, WIDTH), F32),
        vm((ROWS, WIDTH), F32),
        dma((24,)),
        dma((3, 2, 4, 2)), dma((3, 2, 4, 2)),
        dma((3, 8)), dma((3, 8)),
        dma((6, 2)), dma((6, 2)),
        dma((6, 2, 2)), dma((6, 2, 2)),
        dma((4, 2, 4)), dma((4, 2, 4)),
        dma((3,)), dma((3,)),
        dma((4,)), dma((4,)),
        dma((4,)), dma((4,)),
        dma((3,)), dma((3,)),
        dma((2, 4)), dma((2, 4)),
        dma(()), dma(()),
        dma((8,)), dma((8,)),
        dma((8,)), dma((8,)),
        dma((3,)), dma((3,)),
    ]
    hbm = pl.BlockSpec(memory_space=pl.ANY)
    whole = pl.BlockSpec(memory_space=pltpu.VMEM)
    smem = pl.BlockSpec(memory_space=pltpu.SMEM)
    hidden, backed = pl.pallas_call(
        kernel,
        out_shape=(
            pltpu.VMEM((SLOTS, BLK, WIDTH), BF16),
            pltpu.VMEM((1, 128), F32),
        ),
        in_specs=[hbm, hbm, hbm, hbm, hbm, whole, whole, smem, smem],
        out_specs=(whole, whole),
        scratch_shapes=scratch,
        compiler_params=pltpu.CompilerParams(
            collective_id=0, has_side_effects=True, vmem_limit_bytes=56 * 1024 * 1024
        ),
    )(
        queries, keys, values, resid, out_weight,
        norm_gain, value_weight, parent, counts,
    )
    return (hidden, backed[0, :SLOTS])


def solution(mesh):
    in_specs = (
        P("leaf", None, "tensor"),
        P("leaf", None, "tensor"),
        P("leaf", None, "tensor"),
        P("leaf", None, "tensor"),
        P("tensor", None),
        P("tensor"),
        P("tensor"),
        P("leaf"),
        P("leaf"),
    )
    out_specs = (P("leaf", None, "tensor"), P("leaf"))
    return jax.shard_map(body, mesh=mesh, in_specs=in_specs, out_specs=out_specs, check_vma=False)
```

```python
import math

import jax
import jax.numpy as jnp
from jax import lax
from jax.experimental import pallas as pl
from jax.experimental.pallas import tpu as pltpu
from jax.sharding import PartitionSpec as P

D = 4096
DH = 128
BLK = 32
LEVELS = 4
W = 8
NX, NY, NZ, NC = 4, 4, 8, 2
ZC = NZ * NC
SLOTS = LEVELS * W
HEADS_HERE = 4
ROWS = W * BLK
COLS = HEADS_HERE * DH
WIDTH = D // NX
WROWS = COLS // (NY * NC)
TILE = 256
HALF = W // 2
GROUP = 4
BATCHES = ((0, 1), (0, 2), (1, 2), (0, 3), (1, 3), (2, 3))

norm_eps = 1e-05
masked_score = -1e30
BF16 = jnp.bfloat16
F32 = jnp.float32
MESH = pl.DeviceIdType.MESH


def kernel(
    q_hbm, k_hbm, v_hbm, r_hbm, w_hbm, gain_ref, vw_ref, parent_ref, counts_ref,
    hid_v, bk_ref,
    q_v, k_v, v_v, r_v, wf, kvg0, kvg1, kvg2, ag, ysa, ysp, ysm, yh, yr,
    ptl, pyr, pbuf, gr, gyr, psm, pvm, amat, bmat, invm, keepm, stats, srecv, rtile, sqacc, mxacc, mix, partial,
    lsem, zs, zr, sbs, sbr, yas, yar, yfs, yfr, xs, xr, wxs, wxr, wys, wyr, wbs, wbr,
    pys, pyrv, ps, pr, pbs, pbr, gys, gyrv, gs, grv, sts, strv,
):
    kvg = (kvg0, kvg1, kvg2)
    leaf = lax.axis_index("leaf")
    x = lax.axis_index("tensor")
    c = lax.rem(leaf, NC)
    z = lax.rem(leaf // NC, NZ)
    y = leaf // ZC
    zc = lax.rem(leaf, ZC)

    def leaf_of(yy, zz, cc):
        return (yy * NZ + zz) * NC + cc

    def shift(v, d, n):
        return lax.rem(v + d + n, n)

    yp, ym, ya2 = shift(y, 1, NY), shift(y, -1, NY), shift(y, 2, NY)
    xp, xm, xa = shift(x, 1, NX), shift(x, -1, NX), shift(x, 2, NX)
    zp, zm = shift(z, 1, NZ), shift(z, -1, NZ)
    at_zp, at_zm = (leaf_of(y, zp, c), x), (leaf_of(y, zm, c), x)
    at_sib = (leaf_of(y, z, 1 - c), x)
    at_yp, at_ym, at_ya = (leaf_of(yp, z, c), x), (leaf_of(ym, z, c), x), (leaf_of(ya2, z, c), x)
    at_xp, at_xm, at_xa = (leaf, xp), (leaf, xm), (leaf, xa)

    started = []

    def remote(src, dst, ssem, rsem, dev):
        copy = pltpu.make_async_remote_copy(
            src_ref=src, dst_ref=dst, send_sem=ssem, recv_sem=rsem, device_id=dev, device_id_type=MESH
        )
        return copy

    def send(src, dst, ssem, rsem, dev):
        copy = remote(src, dst, ssem, rsem, dev)
        copy.start()
        started.append(copy)

    def drain():
        for copy in started:
            copy.wait_send()
        started.clear()

    def drain_some(keep):
        while len(started) > keep:
            started.pop(0).wait_send()

    def arrived(ref, ssem, rsem):
        remote(ref, ref, ssem, rsem, at_sib).wait_recv()

    barrier = pltpu.get_barrier_semaphore()
    partners = [at_zp, at_zm, at_sib, at_yp, at_ym, at_ya, at_xp, at_xm, at_xa]
    for dev in partners:
        pl.semaphore_signal(barrier, inc=1, device_id=dev, device_id_type=MESH)

    locals_ = []

    def local(src, dst):
        copy = pltpu.make_async_copy(src, dst, lsem.at[len(locals_)])
        copy.start()
        locals_.append(copy)
        return copy

    own_kv = []
    for l in range(3):
        own_kv.append(
            (
                local(k_hbm.at[pl.ds(W * l, W)], kvg[l].at[zc, 0]),
                local(v_hbm.at[pl.ds(W * l, W)], kvg[l].at[zc, 1]),
            )
        )
    in_q = local(q_hbm, q_v)
    in_k = local(k_hbm, k_v)
    in_v = local(v_hbm, v_v)
    in_w = local(w_hbm.at[:, pl.ds(pl.multiple_of(x * WIDTH, WIDTH), WIDTH)], wf.at[3])
    in_r = local(r_hbm, r_v)
    pl.semaphore_wait(barrier, len(partners))

    sub = lax.broadcasted_iota(jnp.int32, (8, 128), 0)
    ln = lax.broadcasted_iota(jnp.int32, (8, 128), 1)
    mine_sub = sub == c * NY + y
    mine_row = z * 8 + c * NY + y
    y_peers = (at_yp, at_ym, at_ya)

    def p_send():
        row = jnp.zeros((8, 128), jnp.int32)
        for n in range(SLOTS):
            row = jnp.where(ln == n, parent_ref[n], row)
        ptl[...] = jnp.where(mine_sub, row, 0)
        for i, dev in enumerate(y_peers):
            send(ptl, pyr.at[i], pys.at[i], pyrv.at[i], dev)

    def p_start():
        for i in range(3):
            arrived(pyr.at[i], pys.at[i], pyrv.at[i])
        pbuf[c, z] = (ptl[...] + pyr[0]) + (pyr[1] + pyr[2])
        own = pbuf.at[c, z]
        send(own, own, ps.at[0, 0], pr.at[0, 0], at_zp)
        send(own, own, ps.at[1, 0], pr.at[1, 0], at_zm)

    def p_step(s):
        for way, d in ((0, -s), (1, s)):
            one = pbuf.at[c, shift(z, d, NZ)]
            arrived(one, ps.at[way, s - 1], pr.at[way, s - 1])
            if s < 3:
                send(one, one, ps.at[way, s], pr.at[way, s], at_zm if way else at_zp)
            if s == 2 and way == 0:
                send(one, one, ps.at[0, 3], pr.at[0, 3], (leaf_of(y, shift(z, 2, NZ), c), x))
        if s == 3:
            arrived(pbuf.at[c, shift(z, 4, NZ)], ps.at[0, 3], pr.at[0, 3])
            send(pbuf.at[c], pbuf.at[c], pbs, pbr, at_sib)

    def p_end():
        arrived(pbuf.at[1 - c], pbs, pbr)
        parents = (pbuf[0] + pbuf[1]).reshape(64, 128)
        pvm[0:64] = parents
        pvm[64:128] = parents
        return local(pvm.at[pl.ds(0, 64)], psm)

    def zidx(d, cc):
        return shift(z, d, NZ) * NC + cc

    def z_start(l, kv):
        own_kv[l][kv].wait()
        own = kvg[l].at[zc, kv]
        send(own, own, zs.at[l, 0, 0, kv], zr.at[l, 0, 0, kv], at_zp)
        send(own, own, zs.at[l, 1, 0, kv], zr.at[l, 1, 0, kv], at_zm)
        if kv == 1:
            own = kvg[l].at[zc]
            send(own, own, sbs.at[l, 0], sbr.at[l, 0], at_sib)

    def z_step(l, kv, s):
        for way, d in ((0, -s), (1, s)):
            if s == 4 and kv != way:
                continue
            shard = kvg[l].at[zidx(d, c)]
            piece = shard.at[kv]
            arrived(piece, zs.at[l, way, s - 1, kv], zr.at[l, way, s - 1, kv])
            if s < 3 or (s == 3 and kv == way):
                send(piece, piece, zs.at[l, way, s, kv], zr.at[l, way, s, kv], at_zm if way else at_zp)
            if kv == 1:
                j = 7 if s == 4 else 1 + way * 3 + s - 1
                send(shard, shard, sbs.at[l, j], sbr.at[l, j], at_sib)

    def z_end(l):
        for j, d in enumerate((0, -1, -2, -3, 1, 2, 3, 4)):
            arrived(kvg[l].at[zidx(d, 1 - c)], sbs.at[l, j], sbr.at[l, j])

    def climb(node, hops):
        for _ in range(hops):
            dev = lax.shift_right_logical(node, 5)
            row = (lax.shift_right_logical(dev, 1) & 7) * 8 + (dev & 1) * NY + lax.shift_right_logical(dev, 4)
            node = jnp.maximum(psm[row, node & 31], 0)
        return node

    def locate(dev, l, n, s):
        node = climb(dev * SLOTS + W * l + n, l - s)
        owner = lax.shift_right_logical(node, 5)
        return lax.shift_right_logical(owner, 4), owner & 15, node & 7

    def y_far(b):
        s, l = BATCHES[b]
        dev = ya2 * ZC + zc

        def pick(n, carry):
            _, src, slot = locate(dev, l, n, s)
            for kv in range(2):
                ysa[b, n, kv] = kvg[s][src, kv, slot]
            return carry

        lax.fori_loop(0, W, pick, 0)
        first, second = ysa.at[b, pl.ds(0, HALF)], ysa.at[b, pl.ds(HALF, HALF)]
        send(first, yh.at[b, 0], yas.at[b, 0], yar.at[b, 0], at_yp)
        send(second, yh.at[b, 1], yas.at[b, 1], yar.at[b, 1], at_ym)

    def y_near(b):
        s, l = BATCHES[b]
        dev_p = yp * ZC + zc
        dev_m = ym * ZC + zc
        for half in range(2):
            arrived(yh.at[b, half], yas.at[b, half], yar.at[b, half])

            def pick(n, carry):
                row = half * HALF + n
                for out, dev, way in ((ysp, dev_p, 0), (ysm, dev_m, 1)):
                    col, src, slot = locate(dev, l, row, s)
                    for kv in range(2):
                        mine = kvg[s][src, kv, slot]
                        if half == way:
                            mine = jnp.where(col == y, mine, yh[b, way, n, kv])
                        out[b, row, kv] = mine
                return carry

            lax.fori_loop(0, HALF, pick, 0)
            rows = pl.ds(half * HALF, HALF)
            send(ysp.at[b, rows], yr.at[b, 0, rows], yfs.at[b, 0, half], yfr.at[b, 0, half], at_yp)
            send(ysm.at[b, rows], yr.at[b, 1, rows], yfs.at[b, 1, half], yfr.at[b, 1, half], at_ym)

    def y_end(b, half):
        rows = pl.ds(half * HALF, HALF)
        for way in range(2):
            arrived(yr.at[b, way, rows], yfs.at[b, way, half], yfr.at[b, way, half])

    row_q = lax.broadcasted_iota(jnp.int32, (HEADS_HERE * BLK, LEVELS * BLK), 0) & (BLK - 1)
    key_j = lax.broadcasted_iota(jnp.int32, (HEADS_HERE * BLK, LEVELS * BLK), 1)

    def attention(l):
        allowed = ((key_j < BLK) & (key_j <= row_q)) | ((key_j >= BLK) & (key_j < BLK * (l + 1)))
        mine_dev = leaf

        def load(n, half):
            node = W * l + n
            q_node = q_v[node]
            q_rows = jnp.concatenate([q_node[:, h * DH : (h + 1) * DH] for h in range(HEADS_HERE)], axis=0)
            parts = [[k_v[node]], [v_v[node]]]
            for k in range(1, l + 1):
                s = l - k
                b = BATCHES.index((s, l))
                col, src, slot = locate(mine_dev, l, n, s)
                here = col == y
                if half == 0:
                    from_p = col == yp
                else:
                    from_p = jnp.logical_not(here | (col == ym))
                for kv in range(2):
                    block = jnp.where(from_p, yr[b, 1, n, kv], yr[b, 0, n, kv])
                    block = jnp.where(here, kvg[s][src, kv, slot], block)
                    parts[kv].append(block)
            for kv in range(2):
                for _ in range(l + 1, LEVELS):
                    parts[kv].append(jnp.zeros((BLK, DH), BF16))
            return q_rows, jnp.concatenate(parts[0], axis=0), jnp.concatenate(parts[1], axis=0)

        def weigh(scores):
            scores = jnp.where(allowed, scores * DH ** (-0.5), masked_score)
            highest = jnp.max(scores, axis=1, keepdims=True)
            expo = jnp.exp(scores - highest)
            return (expo / jnp.sum(expo, axis=1, keepdims=True)).astype(BF16)

        for half in range(2):
            for s in range(l):
                y_end(BATCHES.index((s, l)), half)

            def group(i, carry):
                first = half * HALF + i * GROUP
                loaded = [load(first + j, half) for j in range(GROUP)]
                scores = [
                    lax.dot_general(q, k, (((1,), (1,)), ((), ())), preferred_element_type=F32) for q, k, _ in loaded
                ]
                weights = [weigh(one) for one in scores]
                for j in range(GROUP):
                    got = jnp.dot(weights[j], loaded[j][2], preferred_element_type=F32).astype(BF16)
                    rows = pl.ds(pl.multiple_of((first + j) * BLK, BLK), BLK)
                    for h in range(HEADS_HERE):
                        ag[3, l, rows, h * DH : (h + 1) * DH] = got[h * BLK : (h + 1) * BLK]
                return carry

            lax.fori_loop(0, HALF // GROUP, group, 0)
            rows = pl.ds(half * HALF * BLK, HALF * BLK)
            own = ag.at[3, l, rows]
            send(own, ag.at[0, l, rows], xs.at[l, half, 0], xr.at[l, half, 0], at_xp)
            send(own, ag.at[1, l, rows], xs.at[l, half, 1], xr.at[l, half, 1], at_xm)

    def x_parts(half):
        quarter = HALF * BLK // 2
        return pl.ds(half * 2 * quarter, quarter), pl.ds(half * 2 * quarter + quarter, quarter)

    def x_pass(l, half):
        rows = pl.ds(half * HALF * BLK, HALF * BLK)
        top, low = x_parts(half)
        arrived(ag.at[0, l, rows], xs.at[l, half, 0], xr.at[l, half, 0])
        send(ag.at[0, l, top], ag.at[2, l, top], xs.at[l, half, 2], xr.at[l, half, 2], at_xp)
        arrived(ag.at[1, l, rows], xs.at[l, half, 1], xr.at[l, half, 1])
        send(ag.at[1, l, low], ag.at[2, l, low], xs.at[l, half, 3], xr.at[l, half, 3], at_xm)

    def x_end(l):
        for half in range(2):
            for way, part in enumerate(x_parts(half)):
                arrived(ag.at[2, l, part], xs.at[l, half, 2 + way], xr.at[l, half, 2 + way])

    def w_rows(yy, cc):
        return pl.ds(pl.multiple_of((yy * NC + cc) * WROWS, WROWS), WROWS)

    def w_start():
        rows = w_rows(y, c)
        for slot, to, dev in ((0, xp, at_xp), (1, xm, at_xm), (2, xa, at_xa)):
            cols = pl.ds(pl.multiple_of(to * WIDTH, WIDTH), WIDTH)
            send(w_hbm.at[rows, cols], wf.at[slot, rows], wxs.at[slot], wxr.at[slot], dev)

    three = pl.ds(0, 3)

    def w_mid():
        rows = w_rows(y, c)
        for slot in range(3):
            arrived(wf.at[slot, rows], wxs.at[slot], wxr.at[slot])
        piece = wf.at[three, rows]
        send(piece, piece, wys.at[0], wyr.at[0], at_yp)
        send(piece, piece, wys.at[1], wyr.at[1], at_ym)
        send(piece, piece, wbs.at[0], wbr.at[0], at_sib)

    def w_halves(yy, cc):
        base = (yy * NC + cc) * WROWS
        return (
            pl.ds(pl.multiple_of(base, WROWS // 2), WROWS // 2),
            pl.ds(pl.multiple_of(base + WROWS // 2, WROWS // 2), WROWS // 2),
        )

    def w_pass():
        for j, (yy, dev) in enumerate(((ym, at_yp), (yp, at_ym))):
            piece = wf.at[three, w_rows(yy, c)]
            arrived(piece, wys.at[j], wyr.at[j])
            onward = wf.at[three, w_halves(yy, c)[j]]
            send(onward, onward, wys.at[2 + j], wyr.at[2 + j], dev)
            send(piece, piece, wbs.at[1 + j], wbr.at[1 + j], at_sib)

    def w_last():
        for j in range(2):
            arrived(wf.at[three, w_halves(ya2, c)[j]], wys.at[2 + j], wyr.at[2 + j])
        piece = wf.at[three, w_rows(ya2, c)]
        send(piece, piece, wbs.at[3], wbr.at[3], at_sib)

    def w_end():
        for j, yy in enumerate((y, ym, yp, ya2)):
            arrived(wf.at[three, w_rows(yy, 1 - c)], wbs.at[j], wbr.at[j])
        in_w.wait()

    def project_near(l):
        def tile(j, carry):
            cols = pl.ds(pl.multiple_of(j * TILE, TILE), TILE)
            total = r_v[pl.ds(W * l, W), :, cols].reshape(ROWS, TILE).astype(F32)
            for slot in (3, 0, 1):
                total = total + jnp.dot(ag[slot, l], wf[slot, :, cols], preferred_element_type=F32)
            partial[:, cols] = total
            return carry

        lax.fori_loop(0, WIDTH // TILE, tile, 0)

    def project_far(l):
        sqacc[...] = jnp.zeros_like(sqacc)
        mxacc[...] = jnp.zeros_like(mxacc)

        def tile(j, carry):
            cols = pl.ds(pl.multiple_of(j * TILE, TILE), TILE)
            total = partial[:, cols] + jnp.dot(ag[2, l], wf[2, :, cols], preferred_element_type=F32)
            hid = total.astype(BF16)
            node = W * l + lax.broadcasted_iota(jnp.int32, (W, BLK, TILE), 0)
            hid_v[pl.ds(W * l, W), :, cols] = jnp.where(
                node < counts_ref[0], hid.reshape(W, BLK, TILE), jnp.zeros((W, BLK, TILE), BF16)
            )
            hid_f = hid.astype(F32)
            square = hid_f * hid_f
            mixed = hid_f * mix[:, cols]
            sqacc[...] += square[:, :128] + square[:, 128:]
            mxacc[...] += mixed[:, :128] + mixed[:, 128:]
            return carry

        lax.fori_loop(0, WIDTH // TILE, tile, 0)
        for base, acc in ((0, sqacc), (8, mxacc)):
            for half in range(2):
                turned = acc[half * 128 : (half + 1) * 128].T
                stats[base + 2 * l + half : base + 2 * l + half + 1, :] = jnp.sum(turned, axis=0, keepdims=True)

    def family():
        mix[...] = (gain_ref[...].astype(F32) * vw_ref[...].astype(F32)).reshape(1, WIDTH)
        turned = pvm[...].T
        rows = lax.broadcasted_iota(jnp.int32, (64, 128), 0)
        lanes = lax.broadcasted_iota(jnp.int32, (64, 128), 1)
        first = lax.broadcasted_iota(jnp.int32, (1, 128), 1) < 64
        for l in range(3):
            for j in range(W):
                child = W * (l + 1) + j
                slot = pvm[0:64, child : child + 1] & 31
                bmat[l, j * 64 : (j + 1) * 64, :] = jnp.where(jnp.broadcast_to(slot, (64, 128)) == lanes, 1.0, 0.0)
            for j in range(0, W, 2):
                child = W * (l + 1) + j
                node = jnp.where(first, turned[child : child + 1, :], turned[child + 1 : child + 2, :])
                dev = lax.shift_right_arithmetic(node, 5)
                row = (lax.shift_right_arithmetic(dev, 1) & 7) * 8 + (dev & 1) * NY + lax.shift_right_arithmetic(dev, 4)
                row = jnp.where(node < 0, -1, row)
                amat[l, :, j * 64 : (j + 2) * 64] = jnp.where(
                    jnp.broadcast_to(row, (64, 128)) == rows, 1.0, 0.0
                ).astype(BF16)
            count = jnp.dot(amat[l], bmat[l].astype(BF16), preferred_element_type=F32)
            invm[l] = jnp.where(count > 0, 0.5 / jnp.maximum(count, 1.0), 0.0)
            keepm[l] = jnp.where(count > 0, 0.5, 1.0)

    def tail():
        for i, dev in enumerate((at_xp, at_xm, at_xa)):
            send(stats, srecv.at[i], sts.at[i], strv.at[i], dev)
        drain()
        for i in range(3):
            arrived(srecv.at[i], sts.at[i], strv.at[i])
        total = (stats[...] + srecv[0]) + (srecv[1] + srecv[2])
        score = total[8:16] / jnp.sqrt(total[0:8] / D + norm_eps)
        jj = lax.broadcasted_iota(jnp.int32, (128, 128), 0)
        nn = lax.broadcasted_iota(jnp.int32, (128, 128), 1)
        group = jnp.where((jj // BLK) == (nn & 3), 1.0, 0.0)
        sums = jnp.dot(score, group, preferred_element_type=F32, precision=lax.Precision.HIGHEST)
        per_node = jnp.sum(jnp.where((ln // 4) == sub, sums, 0.0), axis=0, keepdims=True)
        reward = jnp.tanh(per_node / math.sqrt(BLK))
        wide = jnp.broadcast_to(reward, (8, 128))
        rtile[...] = jnp.where(mine_sub & (ln < counts_ref[0]), wide, 0.0)
        for i in range(1, 8):
            yy, cc = shift(y, i // 2, NY), c if i % 2 == 0 else 1 - c
            send(rtile, gyr.at[i], gys.at[i], gyrv.at[i], (leaf_of(yy, z, cc), x))
        for i in range(1, 8):
            arrived(gyr.at[i], gys.at[i], gyrv.at[i])
        merged = rtile[...]
        for i in range(1, 8):
            merged = merged + gyr[i]
        gr[z] = merged
        for i in range(1, NZ):
            send(gr.at[z], gr.at[z], gs.at[i], grv.at[i], (leaf_of(y, shift(z, i, NZ), c), x))
        drain_some(7)
        for i in range(1, NZ):
            arrived(gr.at[shift(z, -i, NZ)], gs.at[i], grv.at[i])
        values = gr[...].reshape(64, 128)
        for l in (2, 1, 0):
            spread = jnp.concatenate(
                [
                    bmat[l, j * 64 : (j + 1) * 64, :]
                    * jnp.broadcast_to(values[:, W * (l + 1) + j : W * (l + 1) + j + 1], (64, 128))
                    for j in range(W)
                ],
                axis=0,
            )
            high = spread.astype(BF16)
            low = (spread - high.astype(F32)).astype(BF16)
            summed = jnp.dot(amat[l], high, preferred_element_type=F32)
            summed = summed + jnp.dot(amat[l], low, preferred_element_type=F32)
            values = keepm[l] * values + invm[l] * summed
        who = lax.broadcasted_iota(jnp.int32, (64, 128), 0)
        bk_ref[...] = jnp.sum(jnp.where(who == mine_row, values, 0.0), axis=0, keepdims=True)

    p_send()
    z_start(0, 0)
    z_start(0, 1)
    z_start(1, 0)
    w_start()
    p_start()
    z_step(0, 0, 1)
    z_step(0, 1, 1)
    p_step(1)
    z_step(1, 0, 1)
    z_start(1, 1)
    in_q.wait()
    in_k.wait()
    in_v.wait()
    attention(0)
    w_mid()
    p_step(2)
    z_step(0, 0, 2)
    z_step(0, 1, 2)
    z_step(1, 0, 2)
    z_step(1, 1, 1)
    p_step(3)
    z_step(0, 0, 3)
    z_step(0, 1, 3)
    z_step(1, 0, 3)
    z_step(1, 1, 2)
    z_start(2, 0)
    z_start(2, 1)
    to_smem = p_end()
    x_pass(0, 0)
    x_pass(0, 1)
    z_step(0, 0, 4)
    z_step(0, 1, 4)
    w_pass()
    z_end(0)
    to_smem.wait()
    y_far(0)
    y_far(1)
    z_step(1, 0, 4)
    z_step(1, 1, 3)
    z_step(2, 0, 1)
    z_step(2, 1, 1)
    y_far(3)
    z_step(1, 1, 4)
    z_step(2, 0, 2)
    z_step(2, 1, 2)
    y_near(0)
    z_end(1)
    y_far(2)
    y_near(1)
    y_far(4)
    z_step(2, 0, 3)
    z_step(2, 1, 3)
    y_near(2)
    attention(1)
    z_step(2, 0, 4)
    z_step(2, 1, 4)
    y_near(3)
    z_end(2)
    y_far(5)
    y_near(4)
    attention(2)
    x_pass(1, 0)
    x_pass(1, 1)
    y_near(5)
    x_pass(2, 0)
    x_pass(2, 1)
    attention(3)
    family()
    in_r.wait()
    w_last()
    w_end()
    project_near(0)
    x_end(0)
    project_far(0)
    x_pass(3, 0)
    project_near(1)
    x_end(1)
    project_far(1)
    project_near(2)
    x_end(2)
    project_far(2)
    x_pass(3, 1)
    project_near(3)
    x_end(3)
    project_far(3)
    tail()
    drain()


def body(queries, keys, values, resid, out_weight, norm_gain, value_weight, parent, counts):
    dma = pltpu.SemaphoreType.DMA
    vm = pltpu.VMEM
    scratch = [
        vm((SLOTS, BLK, COLS), BF16),
        vm((SLOTS, BLK, DH), BF16),
        vm((SLOTS, BLK, DH), BF16),
        vm((SLOTS, BLK, WIDTH), BF16),
        vm((4, COLS, WIDTH), BF16),
        vm((ZC, 2, W, BLK, DH), BF16),
        vm((ZC, 2, W, BLK, DH), BF16),
        vm((ZC, 2, W, BLK, DH), BF16),
        vm((4, LEVELS, ROWS, COLS), BF16),
        vm((6, W, 2, BLK, DH), BF16),
        vm((6, W, 2, BLK, DH), BF16),
        vm((6, W, 2, BLK, DH), BF16),
        vm((6, 2, HALF, 2, BLK, DH), BF16),
        vm((6, 2, W, 2, BLK, DH), BF16),
        vm((8, 128), jnp.int32),
        vm((3, 8, 128), jnp.int32),
        vm((NC, NZ, 8, 128), jnp.int32),
        vm((NZ, 8, 128), F32),
        vm((8, 8, 128), F32),
        pltpu.SMEM((64, 128), jnp.int32),
        vm((128, 128), jnp.int32),
        vm((3, 64, W * 64), BF16),
        vm((3, W * 64, 128), F32),
        vm((3, 64, 128), F32),
        vm((3, 64, 128), F32),
        vm((16, 128), F32),
        vm((3, 16, 128), F32),
        vm((8, 128), F32),
        vm((ROWS, 128), F32),
        vm((ROWS, 128), F32),
        vm((1, WIDTH), F32),
        vm((ROWS, WIDTH), F32),
        dma((24,)),
        dma((3, 2, 4, 2)), dma((3, 2, 4, 2)),
        dma((3, 8)), dma((3, 8)),
        dma((6, 2)), dma((6, 2)),
        dma((6, 2, 2)), dma((6, 2, 2)),
        dma((4, 2, 4)), dma((4, 2, 4)),
        dma((3,)), dma((3,)),
        dma((4,)), dma((4,)),
        dma((4,)), dma((4,)),
        dma((3,)), dma((3,)),
        dma((2, 4)), dma((2, 4)),
        dma(()), dma(()),
        dma((8,)), dma((8,)),
        dma((8,)), dma((8,)),
        dma((3,)), dma((3,)),
    ]
    hbm = pl.BlockSpec(memory_space=pl.ANY)
    whole = pl.BlockSpec(memory_space=pltpu.VMEM)
    smem = pl.BlockSpec(memory_space=pltpu.SMEM)
    hidden, backed = pl.pallas_call(
        kernel,
        out_shape=(
            pltpu.VMEM((SLOTS, BLK, WIDTH), BF16),
            pltpu.VMEM((1, 128), F32),
        ),
        in_specs=[hbm, hbm, hbm, hbm, hbm, whole, whole, smem, smem],
        out_specs=(whole, whole),
        scratch_shapes=scratch,
        compiler_params=pltpu.CompilerParams(
            collective_id=0, has_side_effects=True, vmem_limit_bytes=56 * 1024 * 1024
        ),
    )(
        queries, keys, values, resid, out_weight,
        norm_gain, value_weight, parent, counts,
    )
    return (hidden, backed[0, :SLOTS])


def solution(mesh):
    in_specs = (
        P("leaf", None, "tensor"),
        P("leaf", None, "tensor"),
        P("leaf", None, "tensor"),
        P("leaf", None, "tensor"),
        P("tensor", None),
        P("tensor"),
        P("tensor"),
        P("leaf"),
        P("leaf"),
    )
    out_specs = (P("leaf", None, "tensor"), P("leaf"))
    return jax.shard_map(body, mesh=mesh, in_specs=in_specs, out_specs=out_specs, check_vma=False)
```
